128 devices in a mesh: row: 8 (over x, core), col: 16 (over y, z).
Axes of the slice: x: 4, y: 4, z: 4, core: 2. Of those that a mesh axis runs over, the one named last changes fastest.
Arguments:
- block_input: bfloat16 [1536, 8192], P('col', 'row'), may hold values from -60 to 60
- modulation: float32 [8, 3, 8192], P(None, None, 'row'), may hold values from -3 to 3
- iteration: int32 [1], replicated, may hold values from 0 to 7
- positions: int32 [1536], replicated, may hold values from 0 to 1535, each once
- qkv_weight: bfloat16 [8192, 3, 8192], P('row', None, 'col'), may hold values from -2 to 2
- out_weight: bfloat16 [8192, 8192], P('col', 'row'), may hold values from -0.0625 to 0.0625
- grad_out: bfloat16 [1536, 8192], P('col', 'row'), may hold values from -6 to 6
Outputs:
- grad_input: bfloat16 [1536, 8192], P('col', 'row')
- grad_qkv: bfloat16 [8192, 3, 8192], P('row', None, 'col')
- grad_out_weight: bfloat16 [8192, 8192], P('col', 'row')
- grad_mod: float32 [3, 8192], P(None, 'row')
The draws below stay inside these ranges and needn't reach their ends.
Inputs may be any that keep to these rules, and one draw needn't show every extreme that they name: positions is a permutation of 0 to 1535.
All inputs are finite; a program needn't handle non-finite values.
Results may differ from the reference program's by a relative error of at most 0.0077.
Values may be sent and summed in bfloat16 or wider, within the bound.
A program may use at most 128 MiB of HBM per device.

```python
import math
import jax
import jax.numpy as jnp
from jax import lax

D = 8192
HEADS = 64
HEAD_DIM = 128
LOOPS = 8
TOKENS = 1536


def draw_block_input(key, part):
    key = jax.random.fold_in(key, 11)
    first, second, third = jax.random.split(key, 3)
    base = jax.random.normal(first, (TOKENS, D))
    rows = jnp.exp(jax.random.uniform(second, (TOKENS, 1), minval=0.0, maxval=math.log(10.0)))
    cols = jnp.exp(jax.random.uniform(third, (1, D), minval=0.0, maxval=math.log(10.0)))
    values = base * rows * cols / 10.0
    return jnp.clip(values, -60.0, 60.0).astype(jnp.bfloat16)


def draw_qkv_weight(key, part):
    key = jax.random.fold_in(key, 23)
    first = jax.random.fold_in(key, 0)
    base = jax.random.normal(first, (D, 3, D)) / math.sqrt(D)
    return jnp.clip(base, -2.0, 2.0).astype(jnp.bfloat16)


def levels(own_key, extent, cuts, least, top_value):
    level, own = 1.0, jax.random.fold_in(own_key, 6)
    for position, blocks in cuts:
        heights = jnp.exp(jax.random.uniform(jax.random.fold_in(own, position), (blocks,), jnp.float32, least / len(cuts), top_value / len(cuts)))
        level = level * jnp.repeat(heights, extent[position] // blocks).reshape([-1 if axis == position else 1 for axis in range(len(extent))])
    return level


def noise(own_key, shape, deviation, limit, shards=(), dtype=jnp.bfloat16):
    entries = deviation * jax.random.normal(own_key, shape, jnp.float32)
    if shards:
        entries = entries * levels(own_key, shape, shards, -0.22, 0.18)
    return jnp.clip(entries, -limit, limit).astype(dtype)


def setup_inputs(seed: int = 0) -> dict:
    key_of = jax.random.split(jax.random.key(seed), 8)
    return {
        "block_input": draw_block_input(jax.random.fold_in(key_of[7], 71), 0),
        "modulation": noise(key_of[1], (LOOPS, 3, D), 0.5, 3.0, ((2, 8),), jnp.float32),
        "iteration": jax.random.randint(key_of[2], (1,), 0, LOOPS).astype(jnp.int32),
        "positions": jax.random.permutation(key_of[3], TOKENS).astype(jnp.int32),
        "qkv_weight": draw_qkv_weight(jax.random.fold_in(key_of[7], 71), 0),
        "out_weight": noise(key_of[5], (D, D), D ** -0.5, 0.0625, ((0, 16), (1, 8))),
        "grad_out": noise(key_of[6], (TOKENS, D), 1.0, 6.0, ((0, 16), (1, 8))),
    }


EPS = 1e-06

def reference(block_input, modulation, iteration, positions, qkv_weight, out_weight, grad_out):
    chosen = lax.dynamic_index_in_dim(modulation, iteration[0], 0, keepdims=False)
    shift, scale, gate = (chosen[0], chosen[1], chosen[2])
    x_float = block_input.astype(jnp.float32)
    inv_rms = lax.rsqrt(lax.optimization_barrier(jnp.sum(x_float * x_float, axis=1)) / D + EPS)
    x_hat = x_float * inv_rms[:, None]
    normed = (x_hat * (1.0 + scale) + shift).astype(jnp.bfloat16)
    w_flat = qkv_weight.reshape(D, 3 * D)
    qkv = jnp.dot(normed, w_flat, preferred_element_type=jnp.float32).astype(jnp.bfloat16)
    grad_float = grad_out.astype(jnp.float32)
    grad_z = (grad_float * gate).astype(jnp.bfloat16)
    grad_ctx = jnp.dot(grad_z, out_weight.T, preferred_element_type=jnp.float32).astype(jnp.bfloat16)

    def split_heads(block):
        return block.reshape(TOKENS, HEADS, HEAD_DIM).transpose(1, 0, 2)
    query = split_heads(qkv[:, :D])
    keys = split_heads(qkv[:, D:2 * D])
    values = split_heads(qkv[:, 2 * D:])
    ctx_heads = split_heads(grad_ctx)
    allowed = positions[None, :] <= positions[:, None]
    factor = 1.0 / HEAD_DIM ** 0.5

    def head_step(items):
        q_head, k_head, v_head, g_head = items
        scores = jnp.dot(q_head, k_head.T, preferred_element_type=jnp.float32) * factor
        scores = jnp.where(allowed, scores, -1e+30)
        peak = lax.optimization_barrier(jnp.max(scores, axis=1, keepdims=True))
        weights = jnp.exp(scores - peak)
        probs = weights / lax.optimization_barrier(jnp.sum(weights, axis=1, keepdims=True))
        probs_b = probs.astype(jnp.bfloat16)
        context = jnp.dot(probs_b, v_head, preferred_element_type=jnp.float32).astype(jnp.bfloat16)
        grad_probs = jnp.dot(g_head, v_head.T, preferred_element_type=jnp.float32)
        delta = lax.optimization_barrier(jnp.sum(probs * grad_probs, axis=1, keepdims=True))
        grad_scores = (probs * (grad_probs - delta) * factor).astype(jnp.bfloat16)
        grad_q = jnp.dot(grad_scores, k_head, preferred_element_type=jnp.float32).astype(jnp.bfloat16)
        grad_k = jnp.dot(grad_scores.T, q_head, preferred_element_type=jnp.float32).astype(jnp.bfloat16)
        grad_v = jnp.dot(probs_b.T, g_head, preferred_element_type=jnp.float32).astype(jnp.bfloat16)
        return (context, grad_q, grad_k, grad_v)
    context, grad_q, grad_k, grad_v = lax.map(head_step, (query, keys, values, ctx_heads))

    def join_heads(block):
        return block.transpose(1, 0, 2).reshape(TOKENS, D)
    context = join_heads(context)
    grad_proj = jnp.concatenate([join_heads(grad_q), join_heads(grad_k), join_heads(grad_v)], axis=1)
    z_value = jnp.dot(context, out_weight, preferred_element_type=jnp.float32)
    gate_grad = lax.optimization_barrier(jnp.sum(grad_float * z_value, axis=0))
    grad_out_weight = jnp.dot(context.T, grad_z, preferred_element_type=jnp.float32).astype(jnp.bfloat16)
    grad_qkv = jnp.dot(normed.T, grad_proj, preferred_element_type=jnp.float32).astype(jnp.bfloat16).reshape(D, 3, D)
    grad_normed = jnp.dot(grad_proj, w_flat.T, preferred_element_type=jnp.float32)
    shift_grad = lax.optimization_barrier(jnp.sum(grad_normed, axis=0))
    scale_grad = lax.optimization_barrier(jnp.sum(grad_normed * x_hat, axis=0))
    grad_hat = grad_normed * (1.0 + scale)
    inner = lax.optimization_barrier(jnp.sum(grad_hat * x_hat, axis=1)) / D
    grad_input = ((grad_hat - x_hat * inner[:, None]) * inv_rms[:, None] + grad_float).astype(jnp.bfloat16)
    grad_mod = jnp.stack([shift_grad, scale_grad, gate_grad], axis=0)
    return (grad_input, grad_qkv, grad_out_weight, grad_mod)
```

```python
import functools
import jax
import jax.numpy as jnp
from jax import lax
from jax.experimental import pallas as pl
from jax.experimental.pallas import tpu as pltpu
from jax.sharding import PartitionSpec as P

D = 8192
HEAD_DIM = 128
EPS = 1e-06
MESH = pl.DeviceIdType.MESH
BF = jnp.bfloat16
F32 = jnp.float32

CORE = (0, 1, 0, 0)
XP, XM, X2 = (1, 0, 0, 0), (3, 0, 0, 0), (2, 0, 0, 0)
YP, YM, Y2 = (0, 0, 1, 0), (0, 0, 3, 0), (0, 0, 2, 0)
ZP, ZM, Z2 = (0, 0, 0, 1), (0, 0, 0, 3), (0, 0, 0, 2)

G = 4
HALF = 192
F0, F1 = pl.ds(0, 512), pl.ds(512, 512)


def coords():
    row, col = lax.axis_index("row"), lax.axis_index("col")
    return row // 2, row % 2, col // 4, col % 4


def device(step):
    x, k, y, z = coords()
    dx, dk, dy, dz = step
    x, k, y, z = (x + dx) % 4, (k + dk) % 2, (y + dy) % 4, (z + dz) % 4
    return (x * 2 + k, y * 4 + z)


def enter(steps):
    barrier = pltpu.get_barrier_semaphore()
    for step in steps:
        pl.semaphore_signal(barrier, inc=1, device_id=device(step), device_id_type=MESH)
    pl.semaphore_wait(barrier, len(steps))


class Net:
    def __init__(self, send_sem, recv_sem):
        self.send_sem, self.recv_sem, self.copies = send_sem, recv_sem, []

    def send(self, src, dst, step):
        i = len(self.copies)
        copy = pltpu.make_async_remote_copy(
            src_ref=src,
            dst_ref=dst,
            send_sem=self.send_sem.at[i],
            recv_sem=self.recv_sem.at[i],
            device_id=device(step),
            device_id_type=MESH,
        )
        copy.start()
        self.copies.append(copy)
        return copy

    def drain(self):
        for copy in self.copies:
            copy.wait_send()


class Gather:
    def __init__(self, net, buf):
        _, _, y, z = coords()
        self.net, self.buf, self.y, self.z = net, buf, y, z
        self.yp, self.ym, self.y2 = (y + 1) % 4, (y + 3) % 4, (y + 2) % 4
        self.zp, self.zm, self.z2 = (z + 1) % 4, (z + 3) % 4, (z + 2) % 4
        self.first, self.second = {}, {}

    def put(self, ref, step):
        return self.net.send(ref, ref, step)

    def zsend(self, key, g):
        block = self.buf.at[g, self.z, :, F0]
        self.first[key] = (self.put(block, ZP), self.put(block, ZM))

    def zforward(self, key, g):
        up, down = self.first[key]
        up.wait_recv()
        a = self.put(self.buf.at[g, self.zm, pl.ds(0, 48), F0], ZP)
        down.wait_recv()
        b = self.put(self.buf.at[g, self.zp, pl.ds(48, 48), F0], ZM)
        self.second[key] = (a, b)

    def zend(self, key):
        a, b = self.second[key]
        a.wait_recv()
        b.wait_recv()

    def s1(self):
        f0, f1 = self.buf.at[self.y, self.z, :, F0], self.buf.at[self.y, self.z, :, F1]
        self.a, self.b = self.put(f0, YP), self.put(f0, YM)
        self.c, self.d = self.put(f1, ZP), self.put(f1, ZM)
        self.zsend("own", self.y)

    def s2(self):
        self.c.wait_recv()
        self.c2 = self.put(self.buf.at[self.y, self.zm, pl.ds(0, 48), F1], ZP)
        self.d.wait_recv()
        self.d2 = self.put(self.buf.at[self.y, self.zp, pl.ds(48, 48), F1], ZM)
        self.a.wait_recv()
        self.a2 = self.put(self.buf.at[self.ym, self.z, pl.ds(0, 48), F0], YP)
        self.zsend("ym", self.ym)
        self.b.wait_recv()
        self.b2 = self.put(self.buf.at[self.yp, self.z, pl.ds(48, 48), F0], YM)
        self.zsend("yp", self.yp)

    def s3(self):
        self.c2.wait_recv()
        self.d2.wait_recv()
        group = self.buf.at[self.y, :, :, F1]
        self.gp, self.gm = self.put(group, YP), self.put(group, YM)
        self.zforward("own", self.y)
        self.zend("own")

    def s4(self):
        self.a2.wait_recv()
        self.b2.wait_recv()
        self.zsend("y2", self.y2)
        self.zforward("ym", self.ym)
        self.zforward("yp", self.yp)
        self.gp.wait_recv()
        self.gp2 = self.put(self.buf.at[self.ym, pl.ds(0, 2), :, F1], YP)
        self.gm.wait_recv()
        self.gm2 = self.put(self.buf.at[self.yp, pl.ds(2, 2), :, F1], YM)
        self.zend("ym")
        self.zend("yp")

    def s5(self):
        self.zforward("y2", self.y2)
        self.zend("y2")
        self.gp2.wait_recv()
        self.gm2.wait_recv()


class RowReduce:
    def __init__(self, net, part, sib, hop, hop_in, out_buf, in_buf, w):
        self.net, self.part, self.sib, self.hop, self.hop_in = net, part, sib, hop, hop_in
        self.out_buf, self.in_buf, self.w = out_buf, in_buf, w
        self.x, self.k, _, _ = coords()
        self.c, self.h, self.f = {}, {}, {}

    def start(self, s):
        self.c[s] = self.net.send(self.part.at[s, 1 - self.k], self.sib.at[s], CORE)

    def local(self, s, d, rows):
        cols = pl.ds(d * self.w, self.w)
        return self.part[s, self.k, rows, cols].astype(F32) + self.sib[s, rows, cols].astype(F32)

    def r1(self, s):
        self.c[s].wait_recv()
        self.hop[s] = self.local(s, 0, pl.ds(0, HALF)).astype(BF)
        self.h[s] = (
            self.net.send(self.hop.at[s, pl.ds(0, 96)], self.hop_in.at[s, 0], XP),
            self.net.send(self.hop.at[s, pl.ds(96, 96)], self.hop_in.at[s, 1], XM),
        )

    def r2(self, s):
        a, b = self.h[s]
        lo, hi = pl.ds(0, 96), pl.ds(96, 96)
        self.out_buf[s, 0, hi] = self.local(s, 1, hi).astype(BF)
        self.out_buf[s, 1, lo] = self.local(s, 2, lo).astype(BF)
        a.wait_recv()
        self.out_buf[s, 0, lo] = (self.local(s, 1, lo) + self.hop_in[s, 0].astype(F32)).astype(BF)
        up = self.net.send(self.out_buf.at[s, 0], self.in_buf.at[s, 0], XP)
        b.wait_recv()
        self.out_buf[s, 1, hi] = (self.local(s, 2, hi) + self.hop_in[s, 1].astype(F32)).astype(BF)
        down = self.net.send(self.out_buf.at[s, 1], self.in_buf.at[s, 1], XM)
        self.f[s] = (up, down)

    def r3(self, s):
        own = self.local(s, 3, pl.ds(0, HALF))
        for copy in self.f[s]:
            copy.wait_recv()
        return (own + self.in_buf[s, 0].astype(F32) + self.in_buf[s, 1].astype(F32)).astype(BF)


def row_sum(net, mine, got, value):
    mine[0] = jnp.broadcast_to(value, (96, 128))
    net.send(mine.at[0], got.at[0], CORE).wait_recv()
    mine[1] = mine[0] + got[0]
    copies = [net.send(mine.at[1], got.at[1 + i], step) for i, step in enumerate((XP, XM, X2))]
    for copy in copies:
        copy.wait_recv()
    return (mine[1] + got[1]) + (got[2] + got[3])


def heads_of(x):
    return ((x + 2) % 4, (x + 1) % 4, (x + 3) % 4, x)


def load_weights(wq_hbm, wo_hbm, wv, wo, sem):
    x, _, _, _ = coords()
    copies = []
    for d, head in enumerate(heads_of(x)):
        cols = pl.ds(pl.multiple_of(head * 128, 128), 128)
        for j in range(3):
            copies.append((wq_hbm.at[j, :, cols], wv.at[:, pl.ds(d * 384 + j * 128, 128)]))
        copies.append((wo_hbm.at[cols, :], wo.at[pl.ds(d * 128, 128)]))
    copies = [pltpu.make_async_copy(a, b, sem.at[i]) for i, (a, b) in enumerate(copies)]
    for copy in copies:
        copy.start()
    return copies


NA = 28 * 2 + 5 * 4 * 2 + 4


def project_kernel(
    x_ref, gout_ref, mod_ref, it_ref, wq_hbm, wo_hbm,
    nf, gf, qkvg, inv_ref,
    wv, wo, pq, rq, hq, hqi, oq, iq, pg, rg, hg, hgi, og, ig, mine, got,
    send_sem, recv_sem, load_sem,
):
    x, k, y, z = coords()
    net = Net(send_sem, recv_sem)
    loads = load_weights(wq_hbm, wo_hbm, wv, wo, load_sem)
    enter([CORE, XP, XM, X2, YP, YM, ZP, ZM])
    it = it_ref[0]
    shift, scale, gate = [mod_ref[i, pl.ds(it, 1), :] for i in range(3)]
    gf[y, z] = gout_ref[...]
    cot = Gather(net, gf)
    cot.s1()
    xf = x_ref[...].astype(F32)
    squares = row_sum(net, mine, got, jnp.sum(xf * xf, axis=1, keepdims=True))
    inv = lax.rsqrt(squares / D + EPS)
    inv_ref[...] = inv
    nf[y, z] = (xf * inv[:, :1] * (1.0 + scale) + shift).astype(BF)
    act = Gather(net, nf)
    act.s1()
    for copy in loads:
        copy.wait()
    wo[...] = (wo[...].astype(F32) * gate).astype(BF)
    groups = (act.y, act.ym, act.yp, act.y2)
    rows_q = RowReduce(net, pq, rq, hq, hqi, oq, iq, 384)
    rows_g = RowReduce(net, pg, rg, hg, hgi, og, ig, 128)

    def multiply(s):
        a = nf[groups[s]].reshape(384, 1024)
        for n in range(2):
            cols = pl.ds(n * 768, 768)
            r = jnp.dot(a, wv[:, cols], preferred_element_type=F32)
            pq[s, :, :, cols] = r.astype(BF).reshape(2, HALF, 768)
        rows_q.start(s)

    def multiply_g(s):
        a = gf[groups[s]].reshape(384, 1024)
        r = lax.dot_general(a, wo[...], (((1,), (1,)), ((), ())), preferred_element_type=F32)
        pg[s] = r.astype(BF).reshape(2, HALF, 512)
        rows_g.start(s)

    def finish(s):
        qkvg[groups[s], :, pl.ds(0, 384)] = rows_q.r3(s)

    def finish_g(s):
        qkvg[groups[s], :, pl.ds(384, 128)] = rows_g.r3(s)

    act.s2()
    act.s3()
    multiply(0)
    act.s4()
    cot.s2()
    multiply(1)
    rows_q.r1(0)
    multiply(2)
    rows_q.r1(1)
    rows_q.r2(0)
    act.s5()
    cot.s3()
    multiply(3)
    rows_q.r1(2)
    rows_q.r2(1)
    cot.s4()
    multiply_g(0)
    rows_q.r1(3)
    rows_q.r2(2)
    multiply_g(1)
    multiply_g(2)
    rows_g.r1(0)
    rows_q.r2(3)
    cot.s5()
    multiply_g(3)
    rows_g.r1(1)
    rows_g.r1(2)
    rows_g.r2(0)
    rows_g.r1(3)
    rows_g.r2(1)
    finish(0)
    finish(1)
    rows_g.r2(2)
    rows_g.r2(3)
    finish(2)
    finish(3)
    for s in range(4):
        finish_g(s)
    net.drain()


def attend_kernel(
    qkvg, pos_ref, gp, cx, kv, dk, dv, part, part_in, send_sem, recv_sem
):
    x, k, y, z = coords()
    net = Net(send_sem, recv_sem)
    enter([CORE])
    own = qkvg[...].reshape(768, 512)
    kv[k] = own[:, 128:384]
    exchange = net.send(kv.at[k], kv.at[k], CORE)
    key_pos = jnp.concatenate([pos_ref[pl.ds(0, 1), :], pos_ref[pl.ds(1, 1), :]], axis=1)
    query_pos = jnp.broadcast_to(pos_ref[pl.ds(k, 1), :], (128, 768)).T
    exchange.wait_recv()
    keys = kv[:, :, pl.ds(0, 128)].reshape(1536, 128)
    values = kv[:, :, pl.ds(128, 128)].reshape(1536, 128)
    factor = 1.0 / HEAD_DIM**0.5
    nt = (((1,), (1,)), ((), ()))
    tn = (((0,), (0,)), ((), ()))
    for b in range(4):
        rows = slice(b * 192, b * 192 + 192)
        q, g = own[rows, 0:128], own[rows, 384:512]
        scores = lax.dot_general(q, keys, nt, preferred_element_type=F32) * factor
        scores = jnp.where(key_pos <= query_pos[rows, :1], scores, -1e30)
        weights = jnp.exp(scores - jnp.max(scores, axis=1, keepdims=True))
        probs = weights / jnp.sum(weights, axis=1, keepdims=True)
        probs_b = probs.astype(BF)
        cx[b] = jnp.dot(probs_b, values, preferred_element_type=F32).astype(BF)
        grad_probs = lax.dot_general(g, values, nt, preferred_element_type=F32)
        delta = jnp.sum(probs * grad_probs, axis=1, keepdims=True)
        grad_scores = (probs * (grad_probs - delta) * factor).astype(BF)
        gp[b, :, pl.ds(0, 128)] = jnp.dot(grad_scores, keys, preferred_element_type=F32).astype(BF)
        grad_k = lax.dot_general(grad_scores, q, tn, preferred_element_type=F32)
        grad_v = lax.dot_general(probs_b, g, tn, preferred_element_type=F32)
        if b == 0:
            dk[...] = grad_k.reshape(2, 768, 128)
            dv[...] = grad_v.reshape(2, 768, 128)
        else:
            dk[...] += grad_k.reshape(2, 768, 128)
            dv[...] += grad_v.reshape(2, 768, 128)
    part[:, pl.ds(0, 128)] = dk[1 - k].astype(BF)
    part[:, pl.ds(128, 128)] = dv[1 - k].astype(BF)
    net.send(part, part_in, CORE).wait_recv()
    grad_k = dk[k] + part_in[:, pl.ds(0, 128)].astype(F32)
    grad_v = dv[k] + part_in[:, pl.ds(128, 128)].astype(F32)
    gp[:, :, pl.ds(128, 128)] = grad_k.astype(BF).reshape(4, HALF, 128)
    gp[:, :, pl.ds(256, 128)] = grad_v.astype(BF).reshape(4, HALF, 128)
    net.drain()


class RowGather:
    def __init__(self, net, at, w):
        self.net, self.at, self.w = net, at, w

    def cols(self, d, n=1):
        return pl.ds(d * self.w, n * self.w)

    def start(self):
        own = self.at(slice(None), self.cols(3))
        self.up = self.net.send(own, self.at(slice(None), self.cols(2)), XP)
        self.down = self.net.send(own, self.at(slice(None), self.cols(1)), XM)

    def forward(self):
        lo, hi = pl.ds(0, 96), pl.ds(96, 96)
        self.up.wait_recv()
        self.up2 = self.net.send(self.at(lo, self.cols(2)), self.at(lo, self.cols(0)), XP)
        self.down.wait_recv()
        self.down2 = self.net.send(self.at(hi, self.cols(1)), self.at(hi, self.cols(0)), XM)
        near = self.at(slice(None), self.cols(1, 3))
        self.near = self.net.send(near, near, CORE)

    def finish(self):
        self.up2.wait_recv()
        self.down2.wait_recv()
        far = self.at(slice(None), self.cols(0))
        self.far = self.net.send(far, far, CORE)

    def end(self):
        self.near.wait_recv()
        self.far.wait_recv()


class RingReduce:
    def __init__(self, net, up, down, hop_in, last_in):
        self.net, self.up, self.down, self.hop_in, self.last_in = net, up, down, hop_in, last_in

    def far(self, lo, hi):
        self.a = self.net.send(lo, self.hop_in.at[0], self.up)
        self.b = self.net.send(hi, self.hop_in.at[1], self.down)

    def above(self, lo, whole):
        self.a.wait_recv()
        lo[...] = (lo[...].astype(F32) + self.hop_in[0].astype(F32)).astype(BF)
        self.c = self.net.send(whole, self.last_in.at[0], self.up)

    def below(self, hi, whole):
        self.b.wait_recv()
        hi[...] = (hi[...].astype(F32) + self.hop_in[1].astype(F32)).astype(BF)
        self.d = self.net.send(whole, self.last_in.at[1], self.down)

    def last(self, own):
        own = own.astype(F32)
        self.c.wait_recv()
        self.d.wait_recv()
        return own + self.last_in[0].astype(F32) + self.last_in[1].astype(F32)


NC = 6 * 5 + 28 + 4 + 6


def grads_kernel(
    gp_own, cx_own, nf, gf, x_ref, gout_ref, mod_ref, it_ref, inv_ref, wq_hbm, wo_hbm,
    gin, gmod, gqkv, gow,
    wv, wo, gp, cx, gn, yh0, yi0, t0, zh0, zi0, zh1, zi1, t1, yh1, yi1,
    oq, ow, mine, got, sums, sums_in,
    send_sem, recv_sem, load_sem, store_sem,
):
    x, k, y, z = coords()
    net = Net(send_sem, recv_sem)
    loads = load_weights(wq_hbm, wo_hbm, wv, wo, load_sem)
    enter([CORE, XP, XM, X2, YP, YM, Y2, ZP, ZM, Z2])
    it = it_ref[0]
    shift, scale, gate = [mod_ref[i, pl.ds(it, 1), :] for i in range(3)]
    groups = ((y + 2) % 4, (y + 1) % 4, (y + 3) % 4, y)
    zp, zm, z2 = (z + 1) % 4, (z + 3) % 4, (z + 2) % 4
    gp[:, k, :, pl.ds(3 * 384, 384)] = gp_own[...]
    cx[:, k, :, pl.ds(3 * 128, 128)] = cx_own[...]

    def gather_of(s):
        return RowGather(net, lambda rows, cols: gp.at[groups[s], k, rows, cols], 384)

    def at_context(rows, cols):
        return cx.at[:, k, rows, cols]

    moves = [gather_of(s) for s in range(4)]
    context = RowGather(net, at_context, 128)
    ring_y0 = RingReduce(net, YP, YM, yh0, yi0)
    rings_z1 = [RingReduce(net, ZP, ZM, zh1.at[s], zi1.at[s]) for s in range(4)]
    ring_z0 = RingReduce(net, ZP, ZM, zh0, zi0)
    ring_y1 = RingReduce(net, YP, YM, yh1, yi1)
    lo, hi = pl.ds(0, 48), pl.ds(48, 48)

    def multiply(s):
        a = gp[groups[s]].reshape(384, 1536)
        r = lax.dot_general(a, wv[...], (((1,), (1,)), ((), ())), preferred_element_type=F32)
        gn[s] = r.astype(BF).reshape(4, 96, 1024)

    def z1_far(s):
        rings_z1[s].far(gn.at[s, z2, lo, F1], gn.at[s, z2, hi, F1])

    def z1_near(s):
        rings_z1[s].above(gn.at[s, zp, lo, F1], gn.at[s, zp, :, F1])
        rings_z1[s].below(gn.at[s, zm, hi, F1], gn.at[s, zm, :, F1])

    def z1_last(s):
        return rings_z1[s].last(gn[s, z, :, F1])

    moves[0].start()
    moves[1].start()
    moves[0].forward()
    moves[2].start()
    moves[0].finish()
    moves[1].forward()
    moves[3].start()
    for copy in loads:
        copy.wait()
    moves[0].end()
    multiply(0)
    ring_y0.far(gn.at[0, pl.ds(0, 2), :, F0], gn.at[0, pl.ds(2, 2), :, F0])
    z1_far(0)
    moves[1].finish()
    moves[2].forward()
    context.start()
    moves[1].end()
    multiply(1)
    z1_far(1)
    ring_y0.above(gn.at[1, pl.ds(0, 2), :, F0], gn.at[1, :, :, F0])
    z1_near(0)
    moves[2].finish()
    moves[3].forward()
    moves[2].end()
    multiply(2)
    z1_far(2)
    ring_y0.below(gn.at[2, pl.ds(2, 2), :, F0], gn.at[2, :, :, F0])
    z1_near(1)
    t1[0] = z1_last(0).astype(BF)
    ring_y1.far(t1.at[0, lo], t1.at[0, hi])
    moves[3].finish()
    context.forward()
    moves[3].end()
    multiply(3)
    z1_far(3)
    z1_near(2)
    t1[1] = z1_last(1).astype(BF)
    ring_y1.above(t1.at[1, lo], t1.at[1])
    t0[...] = ring_y0.last(gn[3, :, :, F0]).astype(BF)
    ring_z0.far(t0.at[z2, lo], t0.at[z2, hi])
    z1_near(3)
    t1[2] = z1_last(2).astype(BF)
    ring_y1.below(t1.at[2, hi], t1.at[2])
    context.finish()
    ring_z0.above(t0.at[zp, lo], t0.at[zp])
    ring_z0.below(t0.at[zm, hi], t0.at[zm])

    tn = (((0,), (0,)), ((), ()))
    stores = []

    def store(src, dst):
        copy = pltpu.make_async_copy(src, dst, store_sem.at[len(stores)])
        copy.start()
        stores.append(copy)

    heads = heads_of(x)
    all_gp = gp[...].reshape(1536, 1536)
    for m in range(4):
        rows = pl.ds(m * 256, 256)
        left = nf[:, :, :, rows].reshape(1536, 256)
        oq[rows, :] = lax.dot_general(left, all_gp, tn, preferred_element_type=F32).astype(BF)
    for d, head in enumerate(heads):
        cols = pl.ds(pl.multiple_of(head * 128, 128), 128)
        for j in range(3):
            store(oq.at[:, pl.ds(d * 384 + j * 128, 128)], gqkv.at[j, :, cols])

    context.end()
    all_g = gf[...].reshape(1536, 1024)
    gate_grad = jnp.zeros((1, 1024), F32)
    for m in range(2):
        rows = pl.ds(m * 256, 256)
        left = cx[:, :, :, rows].reshape(1536, 256)
        r = lax.dot_general(left, all_g, tn, preferred_element_type=F32)
        gate_grad += jnp.sum(r * wo[rows, :].astype(F32), axis=0, keepdims=True)
        ow[rows, :] = (r * gate).astype(BF)
    for d, head in enumerate(heads):
        store(ow.at[pl.ds(d * 128, 128)], gow.at[pl.ds(pl.multiple_of(head * 128, 128), 128), :])

    t1[3] = z1_last(3).astype(BF)
    grad0 = ring_z0.last(t0[z])
    grad1 = ring_y1.last(t1[3])
    grad = jnp.concatenate([grad0, grad1], axis=1)
    inv = inv_ref[:, pl.ds(0, 1)]
    x_hat = x_ref[...].astype(F32) * inv
    grad_hat = grad * (1.0 + scale)
    sums[0, pl.ds(0, 1)] = jnp.sum(grad, axis=0, keepdims=True)
    sums[0, pl.ds(1, 1)] = jnp.sum(grad * x_hat, axis=0, keepdims=True)
    sums[0, pl.ds(2, 1)] = gate_grad
    sums[0, pl.ds(3, 5)] = jnp.zeros((5, 1024), F32)
    zc = [net.send(sums.at[0], sums_in.at[i], s) for i, s in enumerate((ZP, ZM, Z2))]
    inner = row_sum(net, mine, got, jnp.sum(grad_hat * x_hat, axis=1, keepdims=True))
    for copy in zc:
        copy.wait_recv()
    sums[1] = (sums[0] + sums_in[0]) + (sums_in[1] + sums_in[2])
    yc = [net.send(sums.at[1], sums_in.at[3 + i], s) for i, s in enumerate((YP, YM, Y2))]
    inner = inner[:, :1] / D
    gin[...] = ((grad_hat - x_hat * inner) * inv + gout_ref[...].astype(F32)).astype(BF)
    for copy in yc:
        copy.wait_recv()
    total = (sums[1] + sums_in[3]) + (sums_in[4] + sums_in[5])
    gmod[...] = total[0:3]
    net.drain()
    for copy in stores:
        copy.wait()


VM = pl.BlockSpec(memory_space=pltpu.VMEM)
SM = pl.BlockSpec(memory_space=pltpu.SMEM)
ANY = pl.BlockSpec(memory_space=pl.ANY)


def sems(n):
    return [pltpu.SemaphoreType.DMA((n,)), pltpu.SemaphoreType.DMA((n,))]


def params(cid):
    return pltpu.CompilerParams(
        collective_id=cid, has_side_effects=True, vmem_limit_bytes=60 << 20
    )


def vb(*shape):
    return pltpu.VMEM(shape, BF)


def vf(*shape):
    return pltpu.VMEM(shape, F32)


def sds(shape, dtype=BF):
    return jax.ShapeDtypeStruct(shape, dtype)


def shards(block_input, modulation, iteration, positions, qkv_weight, out_weight, grad_out):
    mod = modulation.transpose(1, 0, 2)
    wq = qkv_weight.transpose(1, 0, 2)
    pos = positions.astype(F32).reshape(4, 2, HALF).transpose(1, 0, 2).reshape(2, 768)

    def rows(w):
        return [
            vb(4, 2, HALF, 4 * w), vb(4, HALF, 4 * w), vb(4, HALF, w),
            vb(4, 2, 96, w), vb(4, 2, HALF, w), vb(4, 2, HALF, w),
        ]

    nf, gf, qkvg, inv = pl.pallas_call(
        project_kernel,
        name="project",
        out_shape=(sds((4, 4, 96, 1024)), sds((4, 4, 96, 1024)), sds((4, HALF, 512)), sds((96, 128), F32)),
        in_specs=[VM, VM, VM, SM, ANY, ANY],
        out_specs=(VM, VM, VM, VM),
        scratch_shapes=[
            vb(1024, 1536), vb(512, 1024), *rows(384), *rows(128), vf(2, 96, 128), vf(4, 96, 128),
            *sems(NA), pltpu.SemaphoreType.DMA((16,)),
        ],
        compiler_params=params(0),
    )(block_input, grad_out, mod, iteration, wq, out_weight)
    gp, cx = pl.pallas_call(
        attend_kernel,
        name="attend",
        out_shape=(sds((4, HALF, 384)), sds((4, HALF, 128))),
        in_specs=[VM, VM],
        out_specs=(VM, VM),
        scratch_shapes=[
            vb(2, 768, 256), vf(2, 768, 128), vf(2, 768, 128), vb(768, 256), vb(768, 256), *sems(2),
        ],
        compiler_params=params(1),
    )(qkvg, pos)
    gin, gmod, gqkv, gow = pl.pallas_call(
        grads_kernel,
        name="grads",
        out_shape=(sds((96, 1024)), sds((3, 1024), F32), sds((3, 1024, 512)), sds((512, 1024))),
        in_specs=[VM, VM, VM, VM, VM, VM, VM, SM, VM, ANY, ANY],
        out_specs=(VM, VM, ANY, ANY),
        scratch_shapes=[
            vb(1024, 1536), vb(512, 1024), vb(4, 2, HALF, 1536), vb(4, 2, HALF, 512), vb(4, 4, 96, 1024),
            vb(2, 2, 96, 512), vb(2, 4, 96, 512), vb(4, 96, 512), vb(2, 48, 512), vb(2, 96, 512),
            vb(4, 2, 48, 512), vb(4, 2, 96, 512), vb(4, 96, 512), vb(2, 48, 512), vb(2, 96, 512),
            vb(1024, 1536), vb(512, 1024), vf(2, 96, 128), vf(4, 96, 128), vf(2, 8, 1024), vf(6, 8, 1024),
            *sems(NC), pltpu.SemaphoreType.DMA((16,)), pltpu.SemaphoreType.DMA((16,)),
        ],
        compiler_params=params(2),
    )(gp, cx, nf, gf, block_input, grad_out, mod, iteration, inv, wq, out_weight)
    return gin, gqkv.transpose(1, 0, 2), gow, gmod


def solution(mesh):
    placed = (
        P("col", "row"),
        P(None, None, "row"),
        P(),
        P(),
        P("row", None, "col"),
        P("col", "row"),
        P("col", "row"),
    )
    return jax.shard_map(
        shards,
        mesh=mesh,
        in_specs=placed,
        out_specs=(P("col", "row"), P("row", None, "col"), P("col", "row"), P(None, "row")),
        check_vma=False,
    )
```

```python
import functools
import jax
import jax.numpy as jnp
from jax import lax
from jax.experimental import pallas as pl
from jax.experimental.pallas import tpu as pltpu
from jax.sharding import PartitionSpec as P

D = 8192
HEAD_DIM = 128
EPS = 1e-06
LOG2E = 1.4426950408889634
MESH = pl.DeviceIdType.MESH
BF = jnp.bfloat16
F32 = jnp.float32

CORE = (0, 1, 0, 0)
XP, XM, X2 = (1, 0, 0, 0), (3, 0, 0, 0), (2, 0, 0, 0)
YP, YM, Y2 = (0, 0, 1, 0), (0, 0, 3, 0), (0, 0, 2, 0)
ZP, ZM, Z2 = (0, 0, 0, 1), (0, 0, 0, 3), (0, 0, 0, 2)

G = 4
HALF = 192
F0, F1 = pl.ds(0, 512), pl.ds(512, 512)


def coords():
    row, col = lax.axis_index("row"), lax.axis_index("col")
    return row // 2, row % 2, col // 4, col % 4


def device(step):
    x, k, y, z = coords()
    dx, dk, dy, dz = step
    x, k, y, z = (x + dx) % 4, (k + dk) % 2, (y + dy) % 4, (z + dz) % 4
    return (x * 2 + k, y * 4 + z)


def enter(steps):
    barrier = pltpu.get_barrier_semaphore()
    for step in steps:
        pl.semaphore_signal(barrier, inc=1, device_id=device(step), device_id_type=MESH)
    pl.semaphore_wait(barrier, len(steps))


class Net:
    def __init__(self, send_sem, recv_sem):
        self.send_sem, self.recv_sem, self.copies = send_sem, recv_sem, []

    def send(self, src, dst, step):
        i = len(self.copies)
        copy = pltpu.make_async_remote_copy(
            src_ref=src,
            dst_ref=dst,
            send_sem=self.send_sem.at[i],
            recv_sem=self.recv_sem.at[i],
            device_id=device(step),
            device_id_type=MESH,
        )
        copy.start()
        self.copies.append(copy)
        return copy

    def drain(self):
        for copy in self.copies:
            copy.wait_send()


class Gather:
    def __init__(self, net, buf):
        _, _, y, z = coords()
        self.net, self.buf, self.y, self.z = net, buf, y, z
        self.yp, self.ym, self.y2 = (y + 1) % 4, (y + 3) % 4, (y + 2) % 4
        self.zp, self.zm, self.z2 = (z + 1) % 4, (z + 3) % 4, (z + 2) % 4
        self.first, self.second = {}, {}

    def put(self, ref, step):
        return self.net.send(ref, ref, step)

    def zsend(self, key, g):
        block = self.buf.at[g, self.z, :, F0]
        self.first[key] = (self.put(block, ZP), self.put(block, ZM))

    def zforward(self, key, g):
        up, down = self.first[key]
        up.wait_recv()
        a = self.put(self.buf.at[g, self.zm, pl.ds(0, 48), F0], ZP)
        down.wait_recv()
        b = self.put(self.buf.at[g, self.zp, pl.ds(48, 48), F0], ZM)
        self.second[key] = (a, b)

    def zend(self, key):
        a, b = self.second[key]
        a.wait_recv()
        b.wait_recv()

    def s1(self):
        f0, f1 = self.buf.at[self.y, self.z, :, F0], self.buf.at[self.y, self.z, :, F1]
        self.a, self.b = self.put(f0, YP), self.put(f0, YM)
        self.c, self.d = self.put(f1, ZP), self.put(f1, ZM)
        self.zsend("own", self.y)

    def s2(self):
        self.c.wait_recv()
        self.c2 = self.put(self.buf.at[self.y, self.zm, pl.ds(0, 48), F1], ZP)
        self.d.wait_recv()
        self.d2 = self.put(self.buf.at[self.y, self.zp, pl.ds(48, 48), F1], ZM)
        self.a.wait_recv()
        self.a2 = self.put(self.buf.at[self.ym, self.z, pl.ds(0, 48), F0], YP)
        self.zsend("ym", self.ym)
        self.b.wait_recv()
        self.b2 = self.put(self.buf.at[self.yp, self.z, pl.ds(48, 48), F0], YM)
        self.zsend("yp", self.yp)

    def s3(self):
        self.c2.wait_recv()
        self.d2.wait_recv()
        group = self.buf.at[self.y, :, :, F1]
        self.gp, self.gm = self.put(group, YP), self.put(group, YM)
        self.zforward("own", self.y)
        self.zend("own")

    def s4a(self):
        self.a2.wait_recv()
        self.b2.wait_recv()
        self.zsend("y2", self.y2)
        self.zforward("ym", self.ym)
        self.zforward("yp", self.yp)

    def s4b(self):
        self.gp.wait_recv()
        self.gp2 = self.put(self.buf.at[self.ym, pl.ds(0, 2), :, F1], YP)
        self.gm.wait_recv()
        self.gm2 = self.put(self.buf.at[self.yp, pl.ds(2, 2), :, F1], YM)

    def s5(self):
        self.zforward("y2", self.y2)
        self.zend("y2")
        self.gp2.wait_recv()
        self.gm2.wait_recv()


class RowReduce:
    def __init__(self, net, own, part, sib, hop, hop_in, out_buf, in_buf, w):
        self.net, self.own, self.part, self.sib = net, own, part, sib
        self.hop, self.hop_in, self.out_buf, self.in_buf, self.w = hop, hop_in, out_buf, in_buf, w
        self.c, self.h, self.f = {}, {}, {}

    def start(self, s):
        self.c[s] = self.net.send(self.part.at[s], self.sib.at[s], CORE)

    def local(self, s, d, rows):
        cols = pl.ds(d * self.w, self.w)
        return self.own[s, rows, cols] + self.sib[s, rows, cols].astype(F32)

    def r1(self, s):
        self.c[s].wait_recv()
        self.hop[s] = self.local(s, 0, pl.ds(0, HALF)).astype(BF)
        self.h[s] = (
            self.net.send(self.hop.at[s, pl.ds(0, 96)], self.hop_in.at[s, 0], XP),
            self.net.send(self.hop.at[s, pl.ds(96, 96)], self.hop_in.at[s, 1], XM),
        )

    def r2(self, s):
        a, b = self.h[s]
        lo, hi = pl.ds(0, 96), pl.ds(96, 96)
        self.out_buf[s, 0, hi] = self.local(s, 1, hi).astype(BF)
        self.out_buf[s, 1, lo] = self.local(s, 2, lo).astype(BF)
        a.wait_recv()
        self.out_buf[s, 0, lo] = (self.local(s, 1, lo) + self.hop_in[s, 0].astype(F32)).astype(BF)
        up = self.net.send(self.out_buf.at[s, 0], self.in_buf.at[s, 0], XP)
        b.wait_recv()
        self.out_buf[s, 1, hi] = (self.local(s, 2, hi) + self.hop_in[s, 1].astype(F32)).astype(BF)
        down = self.net.send(self.out_buf.at[s, 1], self.in_buf.at[s, 1], XM)
        self.f[s] = (up, down)

    def r3(self, s):
        own = self.local(s, 3, pl.ds(0, HALF))
        for copy in self.f[s]:
            copy.wait_recv()
        return (own + self.in_buf[s, 0].astype(F32) + self.in_buf[s, 1].astype(F32)).astype(BF)


OTHERS = [(dx, dk, 0, 0) for dx in range(4) for dk in range(2) if (dx, dk) != (0, 0)]


def row_sum(net, mine, got, value):
    wide = jnp.concatenate([jnp.broadcast_to(value, (96, 128)), jnp.zeros((32, 128), F32)], axis=0)
    mine[...] = wide.T[0:8]
    copies = [net.send(mine, got.at[i], step) for i, step in enumerate(OTHERS)]
    for copy in copies:
        copy.wait_recv()
    total = mine[...]
    for i in range(7):
        total += got[i]
    return jnp.broadcast_to(total[0:1], (128, 128)).T[0:96, 0:1]


def heads_of(x):
    return ((x + 2) % 4, (x + 1) % 4, (x + 3) % 4, x)


def load_weights(wq_hbm, wo_hbm, wv, wo, sem):
    x, _, _, _ = coords()
    copies = []
    for d, head in enumerate(heads_of(x)):
        cols = pl.ds(pl.multiple_of(head * 128, 128), 128)
        for j, place in enumerate((d * 128, 512 + d * 256, 640 + d * 256)):
            copies.append((wq_hbm.at[j, :, cols], wv.at[:, pl.ds(place, 128)]))
        copies.append((wo_hbm.at[cols, :], wo.at[pl.ds(d * 128, 128)]))
    copies = [pltpu.make_async_copy(a, b, sem.at[i]) for i, (a, b) in enumerate(copies)]
    for copy in copies:
        copy.start()
    return copies


class RowGather:
    def __init__(self, net, at, w):
        self.net, self.at, self.w = net, at, w

    def cols(self, d, n=1):
        return pl.ds(d * self.w, n * self.w)

    def start(self):
        own = self.at(slice(None), self.cols(3))
        self.up = self.net.send(own, self.at(slice(None), self.cols(2)), XP)
        self.down = self.net.send(own, self.at(slice(None), self.cols(1)), XM)

    def forward(self):
        lo, hi = pl.ds(0, 96), pl.ds(96, 96)
        self.up.wait_recv()
        self.up2 = self.net.send(self.at(lo, self.cols(2)), self.at(lo, self.cols(0)), XP)
        self.down.wait_recv()
        self.down2 = self.net.send(self.at(hi, self.cols(1)), self.at(hi, self.cols(0)), XM)
        near = self.at(slice(None), self.cols(1, 3))
        self.near = self.net.send(near, near, CORE)

    def finish(self):
        self.up2.wait_recv()
        self.down2.wait_recv()
        far = self.at(slice(None), self.cols(0))
        self.far = self.net.send(far, far, CORE)

    def end(self):
        self.near.wait_recv()
        self.far.wait_recv()


class RingReduce:
    def __init__(self, net, up, down, hop_in, last_in):
        self.net, self.up, self.down, self.hop_in, self.last_in = net, up, down, hop_in, last_in

    def far(self, lo, hi):
        self.a = self.net.send(lo, self.hop_in.at[0], self.up)
        self.b = self.net.send(hi, self.hop_in.at[1], self.down)

    def above(self, lo, whole):
        self.a.wait_recv()
        lo[...] = (lo[...].astype(F32) + self.hop_in[0].astype(F32)).astype(BF)
        self.c = self.net.send(whole, self.last_in.at[0], self.up)

    def below(self, hi, whole):
        self.b.wait_recv()
        hi[...] = (hi[...].astype(F32) + self.hop_in[1].astype(F32)).astype(BF)
        self.d = self.net.send(whole, self.last_in.at[1], self.down)

    def last(self, own):
        own = own.astype(F32)
        self.c.wait_recv()
        self.d.wait_recv()
        return own + self.last_in[0].astype(F32) + self.last_in[1].astype(F32)


NT = (((1,), (1,)), ((), ()))
TN = (((0,), (0,)), ((), ()))
N_COPIES = 28 * 2 + 5 * 4 * 2 + 14 + 4 + 6 * 9 + 1 + 28 + 6


def kernel(
    x_ref, gout_ref, mod_ref, it_ref, pos_ref, wq_hbm, wo_hbm,
    gin, gmod, gqkv, gow,
    nf, gf, qkvg, wv, wo, wog,
    aq, pq, rq, hq, hqi, oq, iq, ag, pg, rg, hg, hgi, og, ig, mine, got, mine2, got2,
    kv, wts, pos_t, stats, dk, dv, part, part_in,
    gpq, gpkv, cx, gnq, gn, yh0, yi0, t0, zh0, zi0, zh1, zi1, t1, yh1, yi1,
    outq, ow, sums, sums_z, sums_y,
    send_sem, recv_sem, load_sem, store_sem,
):
    x, k, y, z = coords()
    net = Net(send_sem, recv_sem)
    loads = load_weights(wq_hbm, wo_hbm, wv, wo, load_sem)
    enter(OTHERS + [YP, YM, Y2, ZP, ZM, Z2])
    it = it_ref[0]
    shift, scale, gate = [mod_ref[i, pl.ds(it, 1), :] for i in range(3)]

    gf[y, z] = gout_ref[...]
    cot = Gather(net, gf)
    cot.s1()
    xf = x_ref[...].astype(F32)
    squares = row_sum(net, mine, got, jnp.sum(xf * xf, axis=1, keepdims=True))
    inv = lax.rsqrt(squares / D + EPS)
    nf[y, z] = (xf * inv * (1.0 + scale) + shift).astype(BF)
    act = Gather(net, nf)
    act.s1()
    for copy in loads:
        copy.wait()
    wog[...] = (wo[...].astype(F32) * gate).astype(BF)
    key_pos = jnp.concatenate([pos_ref[pl.ds(0, 1), :], pos_ref[pl.ds(1, 1), :]], axis=1)
    pos_t[...] = jnp.broadcast_to(pos_ref[pl.ds(k, 1), :], (128, 768)).T.reshape(4, HALF, 128)
    order = (act.y, act.ym, act.yp, act.y2)
    rows_q = RowReduce(net, aq, pq, rq, hq, hqi, oq, iq, 384)
    rows_g = RowReduce(net, ag, pg, rg, hg, hgi, og, ig, 128)

    def half_of(buf, s, h):
        return buf[order[s], pl.ds(2 * h, 2)].reshape(HALF, 1024)

    def multiply(s):
        for h, dst in ((1 - k, pq), (k, aq)):
            a = half_of(nf, s, h)
            r = jnp.dot(a, wv[:, pl.ds(0, 512)], preferred_element_type=F32).astype(dst.dtype)
            for d in range(4):
                dst[s, :, pl.ds(d * 384, 128)] = r[:, d * 128 : d * 128 + 128]
            r = jnp.dot(a, wv[:, pl.ds(512, 1024)], preferred_element_type=F32).astype(dst.dtype)
            for d in range(4):
                dst[s, :, pl.ds(d * 384 + 128, 256)] = r[:, d * 256 : d * 256 + 256]
            if dst is pq:
                rows_q.start(s)

    def multiply_g(s):
        for h, dst in ((1 - k, pg), (k, ag)):
            r = lax.dot_general(half_of(gf, s, h), wog[...], NT, preferred_element_type=F32)
            dst[s] = r.astype(dst.dtype)
            if dst is pg:
                rows_g.start(s)

    swaps = []

    def finish(s):
        r = rows_q.r3(s)
        qkvg[order[s], :, pl.ds(0, 128)] = r[:, 0:128]
        kv[k, order[s]] = r[:, 128:384]
        half = kv.at[k, order[s]]
        swaps.append(net.send(half, half, CORE))

    def finish_g(s):
        qkvg[order[s], :, pl.ds(128, 128)] = rows_g.r3(s)

    act.s2()
    act.s3()
    multiply(0)
    act.s4a()
    rows_q.r1(0)
    act.s4b()
    cot.s2()
    act.zend("ym")
    multiply(1)
    rows_q.r2(0)
    act.zend("yp")
    multiply(2)
    rows_q.r1(1)
    act.s5()
    cot.s3()
    multiply(3)
    rows_q.r1(2)
    rows_q.r2(1)
    finish(0)
    cot.s4a()
    rows_q.r1(3)
    rows_q.r2(2)
    cot.s4b()
    finish(1)
    multiply_g(0)
    rows_q.r2(3)
    cot.zend("ym")
    multiply_g(1)
    rows_g.r1(0)
    finish(2)
    cot.zend("yp")
    multiply_g(2)
    rows_g.r1(1)
    finish(3)
    cot.s5()
    multiply_g(3)
    rows_g.r1(2)
    rows_g.r2(0)
    rows_g.r2(1)

    groups = ((y + 2) % 4, (y + 1) % 4, (y + 3) % 4, y)
    for copy in swaps:
        copy.wait_recv()
    keys = kv[:, :, :, pl.ds(0, 128)].reshape(1536, 128)
    values = kv[:, :, :, pl.ds(128, 128)].reshape(1536, 128)
    factor = 1.0 / HEAD_DIM**0.5

    def attend(s):
        q = qkvg[groups[s], :, pl.ds(0, 128)]
        scores = lax.dot_general(q, keys, NT, preferred_element_type=F32)
        scores = jnp.where(key_pos <= pos_t[groups[s], :, pl.ds(0, 1)], scores, -1e30)
        peak = jnp.max(scores, axis=1, keepdims=True)
        weights = jnp.exp2((scores - peak) * (factor * LOG2E))
        wts[s] = weights
        inverse = 1.0 / jnp.sum(weights, axis=1, keepdims=True)
        stats[s] = jnp.broadcast_to(inverse, (HALF, 128))
        probs_b = (weights * inverse).astype(BF)
        r = jnp.dot(probs_b, values, preferred_element_type=F32)
        cx[groups[s], k, :, pl.ds(384, 128)] = r.astype(BF)

    def attend_grad(s):
        q = qkvg[groups[s], :, pl.ds(0, 128)]
        g = qkvg[groups[s], :, pl.ds(128, 128)]
        weights, inverse = wts[s], stats[s, :, pl.ds(0, 1)]
        probs_b = (weights * inverse).astype(BF)
        grad_probs = lax.dot_general(g, values, NT, preferred_element_type=F32)
        delta = jnp.sum(weights * grad_probs, axis=1, keepdims=True) * inverse
        grad_scores = (weights * (grad_probs - delta) * (inverse * factor)).astype(BF)
        r = jnp.dot(grad_scores, keys, preferred_element_type=F32)
        gpq[groups[s], k, :, pl.ds(384, 128)] = r.astype(BF)
        grad_k = lax.dot_general(grad_scores, q, TN, preferred_element_type=F32)
        grad_v = lax.dot_general(probs_b, g, TN, preferred_element_type=F32)
        if s == 0:
            dk[...] = grad_k.reshape(2, 768, 128)
            dv[...] = grad_v.reshape(2, 768, 128)
        else:
            dk[...] += grad_k.reshape(2, 768, 128)
            dv[...] += grad_v.reshape(2, 768, 128)

    def gather_q(s):
        return RowGather(net, lambda rows, cols: gpq.at[groups[s], k, rows, cols], 128)

    def gather_kv(s):
        return RowGather(net, lambda rows, cols: gpkv.at[groups[s], k, rows, cols], 256)

    moves_q = [gather_q(s) for s in range(4)]
    moves_kv = [gather_kv(s) for s in range(4)]
    context = RowGather(net, lambda rows, cols: cx.at[:, k, rows, cols], 128)

    attend(0)
    rows_g.r1(3)
    rows_g.r2(2)
    finish_g(0)
    finish_g(1)
    attend(1)
    rows_g.r2(3)
    finish_g(2)
    attend(2)
    attend(3)
    context.start()
    finish_g(3)
    attend_grad(0)
    moves_q[0].start()
    context.forward()
    attend_grad(1)
    moves_q[1].start()
    moves_q[0].forward()
    context.finish()
    attend_grad(2)
    moves_q[2].start()
    moves_q[1].forward()
    moves_q[0].finish()
    attend_grad(3)
    part[:, pl.ds(0, 128)] = dk[1 - k].astype(BF)
    part[:, pl.ds(128, 128)] = dv[1 - k].astype(BF)
    swap = net.send(part, part_in, CORE)
    moves_q[3].start()
    moves_q[2].forward()
    moves_q[1].finish()

    stores = []

    def store(src, dst):
        copy = pltpu.make_async_copy(src, dst, store_sem.at[len(stores)])
        copy.start()
        stores.append(copy)

    heads = heads_of(x)
    head_at = [pl.ds(pl.multiple_of(head * 128, 128), 128) for head in heads]
    ring_y0 = RingReduce(net, YP, YM, yh0, yi0)
    rings_z1 = [RingReduce(net, ZP, ZM, zh1.at[s], zi1.at[s]) for s in range(4)]
    ring_z0 = RingReduce(net, ZP, ZM, zh0, zi0)
    ring_y1 = RingReduce(net, YP, YM, yh1, yi1)
    lo, hi = pl.ds(0, 48), pl.ds(48, 48)
    zp, zm, z2 = (z + 1) % 4, (z + 3) % 4, (z + 2) % 4

    def normed_q(s):
        moves_q[s].end()
        a = gpq[groups[s]].reshape(384, 512)
        gnq[s] = lax.dot_general(a, wv[:, pl.ds(0, 512)], NT, preferred_element_type=F32)

    def normed_kv(s):
        moves_kv[s].end()
        a = gpkv[groups[s]].reshape(384, 1024)
        r = lax.dot_general(a, wv[:, pl.ds(512, 1024)], NT, preferred_element_type=F32)
        gn[s] = (gnq[s] + r).astype(BF).reshape(4, 96, 1024)

    def out_weight():
        context.end()
        all_g = gf[...].reshape(1536, 1024)
        gate_grad = jnp.zeros((1, 1024), F32)
        for m in range(2):
            rows = pl.ds(m * 256, 256)
            left = cx[:, :, :, rows].reshape(1536, 256)
            r = lax.dot_general(left, all_g, TN, preferred_element_type=F32)
            gate_grad += jnp.sum(r * wo[rows, :].astype(F32), axis=0, keepdims=True)
            ow[rows, :] = (r * gate).astype(BF)
        for d in range(4):
            store(ow.at[pl.ds(d * 128, 128)], gow.at[head_at[d], :])
        return gate_grad

    def weight_q(m):
        rows = pl.ds(m * 256, 256)
        left = nf[:, :, :, rows].reshape(1536, 256)
        right = gpq[...].reshape(1536, 512)
        r = lax.dot_general(left, right, TN, preferred_element_type=F32)
        outq[rows, pl.ds(0, 512)] = r.astype(BF)

    def weight_kv(m):
        rows = pl.ds(m * 256, 256)
        left = nf[:, :, :, rows].reshape(1536, 256)
        right = gpkv[...].reshape(1536, 1024)
        r = lax.dot_general(left, right, TN, preferred_element_type=F32)
        outq[rows, pl.ds(512, 1024)] = r.astype(BF)

    def z1_far(s):
        rings_z1[s].far(gn.at[s, z2, lo, F1], gn.at[s, z2, hi, F1])

    def z1_near(s):
        rings_z1[s].above(gn.at[s, zp, lo, F1], gn.at[s, zp, :, F1])
        rings_z1[s].below(gn.at[s, zm, hi, F1], gn.at[s, zm, :, F1])

    def z1_last(s):
        return rings_z1[s].last(gn[s, z, :, F1])

    swap.wait_recv()
    for cols, total in ((pl.ds(0, 128), dk), (pl.ds(128, 128), dv)):
        r = (total[k] + part_in[:, cols].astype(F32)).astype(BF)
        gpkv[:, k, :, pl.ds(3 * 256 + cols.start, 128)] = r.reshape(4, HALF, 128)
    moves_kv[0].start()
    moves_q[3].forward()
    moves_q[2].finish()
    moves_kv[1].start()
    normed_q(0)
    moves_kv[0].forward()
    moves_q[3].finish()
    moves_kv[2].start()
    normed_q(1)
    normed_q(2)
    moves_kv[1].forward()
    moves_kv[0].finish()
    moves_kv[3].start()
    normed_q(3)
    gate_grad = out_weight()
    normed_kv(0)
    ring_y0.far(gn.at[0, pl.ds(0, 2), :, F0], gn.at[0, pl.ds(2, 2), :, F0])
    z1_far(0)
    moves_kv[2].forward()
    moves_kv[1].finish()
    normed_kv(1)
    z1_far(1)
    ring_y0.above(gn.at[1, pl.ds(0, 2), :, F0], gn.at[1, :, :, F0])
    z1_near(0)
    moves_kv[3].forward()
    moves_kv[2].finish()
    normed_kv(2)
    z1_far(2)
    ring_y0.below(gn.at[2, pl.ds(2, 2), :, F0], gn.at[2, :, :, F0])
    z1_near(1)
    t1[0] = z1_last(0).astype(BF)
    ring_y1.far(t1.at[0, lo], t1.at[0, hi])
    moves_kv[3].finish()
    weight_q(0)
    weight_q(1)
    normed_kv(3)
    z1_far(3)
    z1_near(2)
    t1[1] = z1_last(1).astype(BF)
    ring_y1.above(t1.at[1, lo], t1.at[1])
    t0[...] = ring_y0.last(gn[3, :, :, F0]).astype(BF)
    ring_z0.far(t0.at[z2, lo], t0.at[z2, hi])
    z1_near(3)
    t1[2] = z1_last(2).astype(BF)
    ring_y1.below(t1.at[2, hi], t1.at[2])
    weight_q(2)
    ring_z0.above(t0.at[zp, lo], t0.at[zp])
    ring_z0.below(t0.at[zm, hi], t0.at[zm])
    weight_q(3)
    t1[3] = z1_last(3).astype(BF)
    weight_kv(0)

    grad0 = ring_z0.last(t0[z])
    grad1 = ring_y1.last(t1[3])
    grad = jnp.concatenate([grad0, grad1], axis=1)
    x_hat = x_ref[...].astype(F32) * inv
    grad_hat = grad * (1.0 + scale)
    sums[0, pl.ds(0, 1)] = jnp.sum(grad, axis=0, keepdims=True)
    sums[0, pl.ds(1, 1)] = jnp.sum(grad * x_hat, axis=0, keepdims=True)
    sums[0, pl.ds(2, 1)] = gate_grad
    sums[0, pl.ds(3, 5)] = jnp.zeros((5, 1024), F32)
    sums_z[z] = sums[0]
    zc = [net.send(sums.at[0], sums_z.at[z], step) for step in (ZP, ZM, Z2)]
    inner = row_sum(net, mine2, got2, jnp.sum(grad_hat * x_hat, axis=1, keepdims=True)) / D
    for copy in zc:
        copy.wait_recv()
    sums[1] = (sums_z[0] + sums_z[1]) + (sums_z[2] + sums_z[3])
    sums_y[y] = sums[1]
    yc = [net.send(sums.at[1], sums_y.at[y], step) for step in (YP, YM, Y2)]
    gin[...] = ((grad_hat - x_hat * inner) * inv + gout_ref[...].astype(F32)).astype(BF)
    for m in range(1, 4):
        weight_kv(m)
    for d in range(4):
        for j, place in enumerate((d * 128, 512 + d * 256, 640 + d * 256)):
            store(outq.at[:, pl.ds(place, 128)], gqkv.at[j, :, head_at[d]])
    for copy in yc:
        copy.wait_recv()
    gmod[...] = ((sums_y[0] + sums_y[1]) + (sums_y[2] + sums_y[3]))[0:3]
    net.drain()
    for copy in stores:
        copy.wait()


VM = pl.BlockSpec(memory_space=pltpu.VMEM)
SM = pl.BlockSpec(memory_space=pltpu.SMEM)
ANY = pl.BlockSpec(memory_space=pl.ANY)


def vb(*shape):
    return pltpu.VMEM(shape, BF)


def vf(*shape):
    return pltpu.VMEM(shape, F32)


def sds(shape, dtype=BF):
    return jax.ShapeDtypeStruct(shape, dtype)


def shards(block_input, modulation, iteration, positions, qkv_weight, out_weight, grad_out):
    mod = modulation.transpose(1, 0, 2)
    wq = qkv_weight.transpose(1, 0, 2)
    pos = positions.astype(F32).reshape(4, 2, HALF).transpose(1, 0, 2).reshape(2, 768)

    def rows(w):
        return [
            vf(4, HALF, 4 * w), vb(4, HALF, 4 * w), vb(4, HALF, 4 * w), vb(4, HALF, w),
            vb(4, 2, 96, w), vb(4, 2, HALF, w), vb(4, 2, HALF, w),
        ]

    gin, gmod, gqkv, gow = pl.pallas_call(
        kernel,
        name="block_backward",
        out_shape=(sds((96, 1024)), sds((3, 1024), F32), sds((3, 1024, 512)), sds((512, 1024))),
        in_specs=[VM, VM, VM, SM, VM, ANY, ANY],
        out_specs=(VM, VM, ANY, ANY),
        scratch_shapes=[
            vb(4, 4, 96, 1024), vb(4, 4, 96, 1024), vb(4, HALF, 256),
            vb(1024, 1536), vb(512, 1024), vb(512, 1024),
            *rows(384), *rows(128), vf(8, 128), vf(7, 8, 128), vf(8, 128), vf(7, 8, 128),
            vb(2, 4, HALF, 256), vf(4, HALF, 1536), vf(4, HALF, 128), vf(4, HALF, 128),
            vf(2, 768, 128), vf(2, 768, 128), vb(768, 256), vb(768, 256),
            vb(4, 2, HALF, 512), vb(4, 2, HALF, 1024), vb(4, 2, HALF, 512),
            vf(4, 384, 1024), vb(4, 4, 96, 1024),
            vb(2, 2, 96, 512), vb(2, 4, 96, 512), vb(4, 96, 512), vb(2, 48, 512), vb(2, 96, 512),
            vb(4, 2, 48, 512), vb(4, 2, 96, 512), vb(4, 96, 512), vb(2, 48, 512), vb(2, 96, 512),
            vb(1024, 1536), vb(512, 1024), vf(2, 8, 1024), vf(4, 8, 1024), vf(4, 8, 1024),
            pltpu.SemaphoreType.DMA((N_COPIES,)), pltpu.SemaphoreType.DMA((N_COPIES,)),
            pltpu.SemaphoreType.DMA((16,)), pltpu.SemaphoreType.DMA((16,)),
        ],
        compiler_params=pltpu.CompilerParams(
            collective_id=0, has_side_effects=True, vmem_limit_bytes=63 << 20
        ),
    )(block_input, grad_out, mod, iteration, pos, wq, out_weight)
    return gin, gqkv.transpose(1, 0, 2), gow, gmod


def solution(mesh):
    placed = (
        P("col", "row"),
        P(None, None, "row"),
        P(),
        P(),
        P("row", None, "col"),
        P("col", "row"),
        P("col", "row"),
    )
    return jax.shard_map(
        shards,
        mesh=mesh,
        in_specs=placed,
        out_specs=(P("col", "row"), P("row", None, "col"), P("col", "row"), P(None, "row")),
        check_vma=False,
    )
```

```python
import functools
import jax
import jax.numpy as jnp
from jax import lax
from jax.experimental import pallas as pl
from jax.experimental.pallas import tpu as pltpu
from jax.sharding import PartitionSpec as P

D = 8192
HEAD_DIM = 128
EPS = 1e-06
LOG2E = 1.4426950408889634
MESH = pl.DeviceIdType.MESH
BF = jnp.bfloat16
F32 = jnp.float32

CORE = (0, 1, 0, 0)
XP, XM, X2 = (1, 0, 0, 0), (3, 0, 0, 0), (2, 0, 0, 0)
YP, YM, Y2 = (0, 0, 1, 0), (0, 0, 3, 0), (0, 0, 2, 0)
ZP, ZM, Z2 = (0, 0, 0, 1), (0, 0, 0, 3), (0, 0, 0, 2)

G = 4
HALF = 192
F0, F1 = pl.ds(0, 512), pl.ds(512, 512)


def coords():
    row, col = lax.axis_index("row"), lax.axis_index("col")
    return row // 2, row % 2, col // 4, col % 4


def device(step):
    x, k, y, z = coords()
    dx, dk, dy, dz = step
    x, k, y, z = (x + dx) % 4, (k + dk) % 2, (y + dy) % 4, (z + dz) % 4
    return (x * 2 + k, y * 4 + z)


def enter(steps):
    barrier = pltpu.get_barrier_semaphore()
    for step in steps:
        pl.semaphore_signal(barrier, inc=1, device_id=device(step), device_id_type=MESH)
    pl.semaphore_wait(barrier, len(steps))


class Net:
    def __init__(self, send_sem, recv_sem):
        self.send_sem, self.recv_sem, self.copies = send_sem, recv_sem, []

    def send(self, src, dst, step):
        i = len(self.copies)
        copy = pltpu.make_async_remote_copy(
            src_ref=src,
            dst_ref=dst,
            send_sem=self.send_sem.at[i],
            recv_sem=self.recv_sem.at[i],
            device_id=device(step),
            device_id_type=MESH,
        )
        copy.start()
        self.copies.append(copy)
        return copy

    def drain(self):
        for copy in self.copies:
            copy.wait_send()


class Line:
    def __init__(self, net, at, up, down, rows):
        self.net, self.at, self.up, self.down, self.half = net, at, up, down, rows // 2
        self.all = pl.ds(0, rows)

    def put(self, step, rows, way):
        ref = self.at(step, rows)
        return self.net.send(ref, ref, way)

    def start(self):
        self.a, self.b = self.put(0, self.all, self.up), self.put(0, self.all, self.down)

    def forward_up(self):
        self.a.wait_recv()
        self.c = self.put(3, pl.ds(0, self.half), self.up)

    def forward_down(self):
        self.b.wait_recv()
        self.d = self.put(1, pl.ds(self.half, self.half), self.down)

    def forward(self):
        self.forward_up()
        self.forward_down()

    def end(self):
        self.c.wait_recv()
        self.d.wait_recv()


class Gather:
    def __init__(self, net, buf):
        _, _, y, z = coords()

        def along_y(zz, cols):
            return Line(net, lambda n, rows: buf.at[(y + n) % 4, zz, rows, cols], YP, YM, 96)

        def along_z(yy, cols):
            return Line(net, lambda n, rows: buf.at[yy, (z + n) % 4, rows, cols], ZP, ZM, 96)

        self.a, self.b = along_y(z, F0), along_z(y, F1)
        self.zs = [along_z((y + n) % 4, F0) for n in range(4)]
        self.ys = [along_y((z + n) % 4, F1) for n in range(4)]

    def s1(self):
        for line in (self.a, self.b, self.zs[0], self.ys[0]):
            line.start()

    def s2(self):
        self.a.forward_up()
        self.zs[3].start()
        self.b.forward_up()
        self.ys[3].start()
        self.a.forward_down()
        self.zs[1].start()
        self.b.forward_down()
        self.ys[1].start()

    def s3(self):
        self.zs[0].forward()
        self.ys[0].forward()
        self.a.end()
        self.zs[2].start()
        self.b.end()
        self.ys[2].start()
        self.zs[0].end()

    def s4(self):
        for n in (3, 1):
            self.zs[n].forward()
            self.ys[n].forward()

    def s5(self):
        self.zs[2].forward()
        self.ys[2].forward()
        self.zs[3].end()
        self.zs[1].end()

    def s6(self):
        self.zs[2].end()
        for line in self.ys:
            line.end()


class RowReduce:
    def __init__(self, net, own, part, sib, hop, hop_in, out_buf, in_buf, w):
        self.net, self.own, self.part, self.sib = net, own, part, sib
        self.hop, self.hop_in, self.out_buf, self.in_buf, self.w = hop, hop_in, out_buf, in_buf, w
        self.c, self.h, self.f = {}, {}, {}

    def start(self, s):
        self.c[s] = self.net.send(self.part.at[s], self.sib.at[s], CORE)

    def local(self, s, d, rows):
        cols = pl.ds(d * self.w, self.w)
        return self.own[s, rows, cols] + self.sib[s, rows, cols].astype(F32)

    def put(self, s, i, rows, way):
        copy = self.net.send(self.out_buf.at[s, i, rows], self.in_buf.at[s, i, rows], way)
        self.f.setdefault(s, []).append(copy)

    def r1(self, s):
        lo, hi = pl.ds(0, 96), pl.ds(96, 96)
        self.c[s].wait_recv()
        self.hop[s] = self.local(s, 0, pl.ds(0, HALF)).astype(BF)
        self.h[s] = (
            self.net.send(self.hop.at[s, lo], self.hop_in.at[s, 0], XP),
            self.net.send(self.hop.at[s, hi], self.hop_in.at[s, 1], XM),
        )
        self.out_buf[s, 0, hi] = self.local(s, 1, hi).astype(BF)
        self.put(s, 0, hi, XP)
        self.out_buf[s, 1, lo] = self.local(s, 2, lo).astype(BF)
        self.put(s, 1, lo, XM)

    def r2(self, s):
        a, b = self.h[s]
        lo, hi = pl.ds(0, 96), pl.ds(96, 96)
        a.wait_recv()
        self.out_buf[s, 0, lo] = (self.local(s, 1, lo) + self.hop_in[s, 0].astype(F32)).astype(BF)
        self.put(s, 0, lo, XP)
        b.wait_recv()
        self.out_buf[s, 1, hi] = (self.local(s, 2, hi) + self.hop_in[s, 1].astype(F32)).astype(BF)
        self.put(s, 1, hi, XM)

    def r3(self, s):
        own = self.local(s, 3, pl.ds(0, HALF))
        for copy in self.f[s]:
            copy.wait_recv()
        return (own + self.in_buf[s, 0].astype(F32) + self.in_buf[s, 1].astype(F32)).astype(BF)


OTHERS = [(dx, dk, 0, 0) for dx in range(4) for dk in range(2) if (dx, dk) != (0, 0)]


class RowSum:
    def __init__(self, net, mine, got, value):
        self.mine, self.got = mine, got
        wide = jnp.concatenate([jnp.broadcast_to(value, (96, 128)), jnp.zeros((32, 128), F32)], axis=0)
        mine[...] = wide.T[0:8]
        self.copies = [net.send(mine, got.at[i], step) for i, step in enumerate(OTHERS)]

    def total(self):
        for copy in self.copies:
            copy.wait_recv()
        total = self.mine[...]
        for i in range(7):
            total += self.got[i]
        return jnp.broadcast_to(total[0:1], (128, 128)).T[0:96, 0:1]


def heads_of(x):
    return ((x + 2) % 4, (x + 1) % 4, (x + 3) % 4, x)


def load_weights(wq_hbm, wo_hbm, wv, wo, sem):
    x, _, _, _ = coords()
    copies = []
    for d, head in enumerate(heads_of(x)):
        cols = pl.ds(pl.multiple_of(head * 128, 128), 128)
        for j, place in enumerate((d * 128, 512 + d * 256, 640 + d * 256)):
            copies.append((wq_hbm.at[j, :, cols], wv.at[:, pl.ds(place, 128)]))
        copies.append((wo_hbm.at[cols, :], wo.at[pl.ds(d * 128, 128)]))
    copies = [pltpu.make_async_copy(a, b, sem.at[i]) for i, (a, b) in enumerate(copies)]
    for copy in copies:
        copy.start()
    return copies


class RowGather:
    def __init__(self, net, at, w):
        self.net, self.at, self.w = net, at, w

    def cols(self, d, n=1):
        return pl.ds(d * self.w, n * self.w)

    def start(self):
        own = self.at(slice(None), self.cols(3))
        self.up = self.net.send(own, self.at(slice(None), self.cols(2)), XP)
        self.down = self.net.send(own, self.at(slice(None), self.cols(1)), XM)

    def forward(self):
        lo, hi = pl.ds(0, 96), pl.ds(96, 96)
        self.up.wait_recv()
        self.up2 = self.net.send(self.at(lo, self.cols(2)), self.at(lo, self.cols(0)), XP)
        self.down.wait_recv()
        self.down2 = self.net.send(self.at(hi, self.cols(1)), self.at(hi, self.cols(0)), XM)
        near = self.at(slice(None), self.cols(1, 3))
        self.near = self.net.send(near, near, CORE)

    def finish(self):
        self.up2.wait_recv()
        self.down2.wait_recv()
        far = self.at(slice(None), self.cols(0))
        self.far = self.net.send(far, far, CORE)

    def end(self):
        self.near.wait_recv()
        self.far.wait_recv()


class RingReduce:
    def __init__(self, net, up, down, hop_in, last_in, lo, hi):
        self.net, self.up, self.down, self.hop_in, self.last_in = net, up, down, hop_in, last_in
        self.lo, self.hi, self.tail = lo, hi, []

    def far(self, chunk):
        self.a = self.net.send(chunk.at[self.lo], self.hop_in.at[0], self.up)
        self.b = self.net.send(chunk.at[self.hi], self.hop_in.at[1], self.down)

    def put(self, chunk, i, rows, way):
        self.tail.append(self.net.send(chunk.at[rows], self.last_in.at[i].at[rows], way))

    def above_now(self, chunk):
        self.put(chunk, 0, self.hi, self.up)

    def below_now(self, chunk):
        self.put(chunk, 1, self.lo, self.down)

    def above(self, chunk):
        part = chunk.at[self.lo]
        self.a.wait_recv()
        part[...] = (part[...].astype(F32) + self.hop_in[0].astype(F32)).astype(BF)
        self.put(chunk, 0, self.lo, self.up)

    def below(self, chunk):
        part = chunk.at[self.hi]
        self.b.wait_recv()
        part[...] = (part[...].astype(F32) + self.hop_in[1].astype(F32)).astype(BF)
        self.put(chunk, 1, self.hi, self.down)

    def last(self, own):
        own = own.astype(F32)
        for copy in self.tail:
            copy.wait_recv()
        return own + self.last_in[0].astype(F32) + self.last_in[1].astype(F32)


NT = (((1,), (1,)), ((), ()))
TN = (((0,), (0,)), ((), ()))
N_COPIES = 40 * 2 + 7 * 4 * 2 + 14 + 4 + 6 * 9 + 1 + 42 + 6


def kernel(
    x_ref, gout_ref, mod_ref, it_ref, pos_ref, wq_hbm, wo_hbm,
    gin, gmod, gqkv, gow,
    nf, gf, qkvg, wv, wo, wog,
    aq, pq, rq, hq, hqi, oq, iq, ag, pg, rg, hg, hgi, og, ig, mine, got, mine2, got2,
    kv, wts, pos_t, stats, dk, dv, part, part_in,
    gpq, gpkv, cx, gnq, gn, yh0, yi0, t0, zh0, zi0, zh1, zi1, t1, yh1, yi1,
    outq, ow, sums, sums_z, sums_y,
    send_sem, recv_sem, load_sem, store_sem,
):
    x, k, y, z = coords()
    net = Net(send_sem, recv_sem)
    loads = load_weights(wq_hbm, wo_hbm, wv, wo, load_sem)
    enter(OTHERS + [YP, YM, Y2, ZP, ZM, Z2])
    it = it_ref[0]
    shift, scale, gate = [mod_ref[i, pl.ds(it, 1), :] for i in range(3)]

    gf[y, z] = gout_ref[...]
    cot = Gather(net, gf)
    cot.s1()
    xf = x_ref[...].astype(F32)
    squares = RowSum(net, mine, got, jnp.sum(xf * xf, axis=1, keepdims=True))
    for copy in loads:
        copy.wait()
    wog[...] = (wo[...].astype(F32) * gate).astype(BF)
    key_pos = jnp.concatenate([pos_ref[pl.ds(2 * g + h, 1), :] for h in range(2) for g in range(4)], axis=1)
    for g in range(4):
        pos_t[g] = jnp.broadcast_to(pos_ref[pl.ds(2 * g + k, 1), :], (128, HALF)).T
    inv = lax.rsqrt(squares.total() / D + EPS)
    nf[y, z] = (xf * inv * (1.0 + scale) + shift).astype(BF)
    act = Gather(net, nf)
    act.s1()
    order = (y, (y + 3) % 4, (y + 1) % 4, (y + 2) % 4)
    rows_q = RowReduce(net, aq, pq, rq, hq, hqi, oq, iq, 384)
    rows_g = RowReduce(net, ag, pg, rg, hg, hgi, og, ig, 128)

    def half_of(buf, s, h):
        return buf[order[s], pl.ds(2 * h, 2)].reshape(HALF, 1024)

    def multiply(s):
        for h, dst in ((1 - k, pq), (k, aq)):
            a = half_of(nf, s, h)
            r = jnp.dot(a, wv[:, pl.ds(0, 512)], preferred_element_type=F32).astype(dst.dtype)
            for d in range(4):
                dst[s, :, pl.ds(d * 384, 128)] = r[:, d * 128 : d * 128 + 128]
            r = jnp.dot(a, wv[:, pl.ds(512, 1024)], preferred_element_type=F32).astype(dst.dtype)
            for d in range(4):
                dst[s, :, pl.ds(d * 384 + 128, 256)] = r[:, d * 256 : d * 256 + 256]
            if dst is pq:
                rows_q.start(s)

    def multiply_g(s):
        for h, dst in ((1 - k, pg), (k, ag)):
            r = lax.dot_general(half_of(gf, s, h), wog[...], NT, preferred_element_type=F32)
            dst[s] = r.astype(dst.dtype)
            if dst is pg:
                rows_g.start(s)

    swaps = []

    def finish(s):
        r = rows_q.r3(s)
        qkvg[order[s], :, pl.ds(0, 128)] = r[:, 0:128]
        kv[k, order[s]] = r[:, 128:384]
        half = kv.at[k, order[s]]
        swaps.append(net.send(half, half, CORE))

    def finish_g(s):
        qkvg[order[s], :, pl.ds(128, 128)] = rows_g.r3(s)

    act.s2()
    act.s3()
    multiply(0)
    act.s4()
    cot.s2()
    rows_q.r1(0)
    act.s5()
    multiply(1)
    cot.s3()
    rows_q.r2(0)
    multiply(2)
    rows_q.r1(1)
    act.s6()
    cot.s4()
    multiply(3)
    rows_q.r1(2)
    rows_q.r2(1)
    multiply_g(0)
    cot.s5()
    rows_q.r1(3)
    finish(0)
    rows_q.r2(2)
    multiply_g(1)
    multiply_g(2)
    cot.s6()
    rows_q.r2(3)
    rows_g.r1(0)
    multiply_g(3)
    finish(1)
    rows_g.r1(1)
    rows_g.r1(2)
    finish(2)
    rows_g.r2(0)
    rows_g.r1(3)
    finish(3)
    rows_g.r2(1)

    groups = ((y + 2) % 4, (y + 1) % 4, (y + 3) % 4, y)
    for copy in swaps:
        copy.wait_recv()
    keys = kv[:, :, :, pl.ds(0, 128)].reshape(1536, 128)
    values = kv[:, :, :, pl.ds(128, 128)].reshape(1536, 128)
    factor = 1.0 / HEAD_DIM**0.5

    def attend(s):
        q = qkvg[groups[s], :, pl.ds(0, 128)]
        scores = lax.dot_general(q, keys, NT, preferred_element_type=F32)
        scores = jnp.where(key_pos <= pos_t[groups[s], :, pl.ds(0, 1)], scores, -1e30)
        peak = jnp.max(scores, axis=1, keepdims=True)
        weights = jnp.exp2((scores - peak) * (factor * LOG2E))
        wts[s] = weights
        inverse = 1.0 / jnp.sum(weights, axis=1, keepdims=True)
        stats[s] = jnp.broadcast_to(inverse, (HALF, 128))
        probs_b = (weights * inverse).astype(BF)
        r = jnp.dot(probs_b, values, preferred_element_type=F32)
        cx[groups[s], k, :, pl.ds(384, 128)] = r.astype(BF)

    def attend_grad(s):
        q = qkvg[groups[s], :, pl.ds(0, 128)]
        g = qkvg[groups[s], :, pl.ds(128, 128)]
        weights, inverse = wts[s], stats[s, :, pl.ds(0, 1)]
        probs_b = (weights * inverse).astype(BF)
        grad_probs = lax.dot_general(g, values, NT, preferred_element_type=F32)
        delta = jnp.sum(weights * grad_probs, axis=1, keepdims=True) * inverse
        grad_scores = (weights * (grad_probs - delta) * (inverse * factor)).astype(BF)
        r = jnp.dot(grad_scores, keys, preferred_element_type=F32)
        gpq[groups[s], k, :, pl.ds(384, 128)] = r.astype(BF)
        grad_k = jnp.dot(q.T, grad_scores, preferred_element_type=F32)
        grad_v = jnp.dot(g.T, probs_b, preferred_element_type=F32)
        if s == 0:
            dk[...] = grad_k
            dv[...] = grad_v
        else:
            dk[...] += grad_k
            dv[...] += grad_v

    def gather_q(s):
        return RowGather(net, lambda rows, cols: gpq.at[groups[s], k, rows, cols], 128)

    def gather_kv(s):
        return RowGather(net, lambda rows, cols: gpkv.at[groups[s], k, rows, cols], 256)

    moves_q = [gather_q(s) for s in range(4)]
    moves_kv = [gather_kv(s) for s in range(4)]
    context = RowGather(net, lambda rows, cols: cx.at[:, k, rows, cols], 128)

    attend(0)
    rows_g.r2(2)
    attend(1)
    rows_g.r2(3)
    finish_g(0)
    finish_g(1)
    attend(2)
    finish_g(2)
    attend(3)
    finish_g(3)
    for s in range(4):
        attend_grad(s)
        if s < 3:
            moves_q[s].start()
    mine_at = pl.ds(pl.multiple_of(k * 768, 128), 768)
    theirs_at = pl.ds(pl.multiple_of((1 - k) * 768, 128), 768)
    part[pl.ds(0, 128)] = dk[:, theirs_at].astype(BF)
    part[pl.ds(128, 128)] = dv[:, theirs_at].astype(BF)
    swap = net.send(part, part_in, CORE)
    moves_q[3].start()
    moves_q[0].forward()
    moves_q[1].forward()

    stores = []

    def store(src, dst):
        copy = pltpu.make_async_copy(src, dst, store_sem.at[len(stores)])
        copy.start()
        stores.append(copy)

    heads = heads_of(x)
    head_at = [pl.ds(pl.multiple_of(head * 128, 128), 128) for head in heads]
    lo, hi = pl.ds(0, 48), pl.ds(48, 48)
    ring_y0 = RingReduce(net, YP, YM, yh0, yi0, pl.ds(0, 2), pl.ds(2, 2))
    rings_z1 = [RingReduce(net, ZP, ZM, zh1.at[s], zi1.at[s], lo, hi) for s in range(4)]
    ring_z0 = RingReduce(net, ZP, ZM, zh0, zi0, lo, hi)
    ring_y1 = RingReduce(net, YP, YM, yh1, yi1, lo, hi)
    zp, zm, z2 = (z + 1) % 4, (z + 3) % 4, (z + 2) % 4

    def normed_q(s):
        moves_q[s].end()
        a = gpq[groups[s]].reshape(384, 512)
        gnq[s] = lax.dot_general(a, wv[:, pl.ds(0, 512)], NT, preferred_element_type=F32)

    def normed_kv(s):
        moves_kv[s].end()
        a = gpkv[groups[s]].reshape(384, 1024)
        r = lax.dot_general(a, wv[:, pl.ds(512, 1024)], NT, preferred_element_type=F32)
        gn[s] = (gnq[s] + r).astype(BF).reshape(4, 96, 1024)

    def out_weight():
        context.end()
        all_g = gf[...].reshape(1536, 1024)
        gate_grad = jnp.zeros((1, 1024), F32)
        for m in range(2):
            rows = pl.ds(m * 256, 256)
            left = cx[:, :, :, rows].reshape(1536, 256)
            r = lax.dot_general(left, all_g, TN, preferred_element_type=F32)
            gate_grad += jnp.sum(r * wo[rows, :].astype(F32), axis=0, keepdims=True)
            ow[rows, :] = (r * gate).astype(BF)
        for d in range(4):
            store(ow.at[pl.ds(d * 128, 128)], gow.at[head_at[d], :])
        return gate_grad

    def weight_q(m):
        rows = pl.ds(m * 256, 256)
        left = nf[:, :, :, rows].reshape(1536, 256)
        right = gpq[...].reshape(1536, 512)
        r = lax.dot_general(left, right, TN, preferred_element_type=F32)
        outq[rows, pl.ds(0, 512)] = r.astype(BF)

    def weight_kv(m):
        rows = pl.ds(m * 256, 256)
        left = nf[:, :, :, rows].reshape(1536, 256)
        right = gpkv[...].reshape(1536, 1024)
        r = lax.dot_general(left, right, TN, preferred_element_type=F32)
        outq[rows, pl.ds(512, 1024)] = r.astype(BF)

    def z1_far(s):
        rings_z1[s].far(gn.at[s, z2, :, F1])
        rings_z1[s].above_now(gn.at[s, zp, :, F1])
        rings_z1[s].below_now(gn.at[s, zm, :, F1])

    def z1_near(s):
        rings_z1[s].above(gn.at[s, zp, :, F1])
        rings_z1[s].below(gn.at[s, zm, :, F1])

    def z1_last(s):
        return rings_z1[s].last(gn[s, z, :, F1])

    def rows_of(s):
        return gn.at[s, :, :, F0]

    swap.wait_recv()
    for i, total in ((0, dk), (1, dv)):
        r = total[:, mine_at] + part_in[pl.ds(i * 128, 128)].astype(F32)
        gpkv[:, k, :, pl.ds(768 + i * 128, 128)] = r.T.astype(BF).reshape(4, HALF, 128)
    moves_kv[0].start()
    moves_q[2].forward()
    moves_q[3].forward()
    moves_kv[1].start()
    moves_q[0].finish()
    moves_q[1].finish()
    normed_q(0)
    moves_q[2].finish()
    moves_kv[0].forward()
    moves_kv[2].start()
    moves_q[3].finish()
    normed_q(1)
    normed_q(2)
    moves_kv[1].forward()
    moves_kv[3].start()
    normed_q(3)
    moves_kv[0].finish()
    weight_q(0)
    normed_kv(0)
    ring_y0.far(rows_of(0))
    z1_far(0)
    moves_kv[2].forward()
    moves_kv[1].finish()
    weight_q(1)
    normed_kv(1)
    ring_y0.above_now(rows_of(1))
    z1_far(1)
    moves_kv[3].forward()
    context.start()
    moves_kv[2].finish()
    z1_near(0)
    normed_kv(2)
    ring_y0.below_now(rows_of(2))
    z1_far(2)
    ring_y0.above(rows_of(1))
    moves_kv[3].finish()
    context.forward()
    z1_near(1)
    normed_kv(3)
    z1_far(3)
    ring_y0.below(rows_of(2))
    t1[0] = z1_last(0).astype(BF)
    ring_y1.far(t1.at[0])
    z1_near(2)
    t1[1] = z1_last(1).astype(BF)
    ring_y1.above_now(t1.at[1])
    z1_near(3)
    weight_q(2)
    ring_y1.above(t1.at[1])
    t1[2] = z1_last(2).astype(BF)
    ring_y1.below_now(t1.at[2])
    ring_y1.below(t1.at[2])
    context.finish()
    weight_q(3)
    t0[...] = ring_y0.last(gn[3, :, :, F0]).astype(BF)
    ring_z0.far(t0.at[z2])
    ring_z0.above_now(t0.at[zp])
    ring_z0.below_now(t0.at[zm])
    gate_grad = out_weight()
    ring_z0.above(t0.at[zp])
    ring_z0.below(t0.at[zm])
    t1[3] = z1_last(3).astype(BF)
    weight_kv(0)
    weight_kv(1)

    grad0 = ring_z0.last(t0[z])
    grad1 = ring_y1.last(t1[3])
    grad = jnp.concatenate([grad0, grad1], axis=1)
    x_hat = x_ref[...].astype(F32) * inv
    grad_hat = grad * (1.0 + scale)
    sums[0, pl.ds(0, 1)] = jnp.sum(grad, axis=0, keepdims=True)
    sums[0, pl.ds(1, 1)] = jnp.sum(grad * x_hat, axis=0, keepdims=True)
    sums[0, pl.ds(2, 1)] = gate_grad
    sums[0, pl.ds(3, 5)] = jnp.zeros((5, 1024), F32)
    sums_z[z] = sums[0]
    zc = [net.send(sums.at[0], sums_z.at[z], step) for step in (ZP, ZM, Z2)]
    inner = RowSum(net, mine2, got2, jnp.sum(grad_hat * x_hat, axis=1, keepdims=True))
    weight_kv(2)
    weight_kv(3)
    for d in range(4):
        for j, place in enumerate((d * 128, 512 + d * 256, 640 + d * 256)):
            store(outq.at[:, pl.ds(place, 128)], gqkv.at[j, :, head_at[d]])
    for copy in zc:
        copy.wait_recv()
    sums[1] = (sums_z[0] + sums_z[1]) + (sums_z[2] + sums_z[3])
    sums_y[y] = sums[1]
    yc = [net.send(sums.at[1], sums_y.at[y], step) for step in (YP, YM, Y2)]
    inner = inner.total() / D
    gin[...] = ((grad_hat - x_hat * inner) * inv + gout_ref[...].astype(F32)).astype(BF)
    for copy in yc:
        copy.wait_recv()
    gmod[...] = ((sums_y[0] + sums_y[1]) + (sums_y[2] + sums_y[3]))[0:3]
    net.drain()
    for copy in stores:
        copy.wait()


def place_kernel(a, b, c, d, oa, ob, oc, od, va, vb_, vc, vd, load_sem, store_sem):
    parts = []
    for src, mid, dst, n in ((a, va, oa, 1), (b, vb_, ob, 1), (c, vc, oc, 6), (d, vd, od, 2)):
        for i in range(n):
            if n == 6:
                at = (i // 2, pl.ds(512 * (i % 2), 512))
            elif n == 2:
                at = (pl.ds(256 * i, 256),)
            else:
                at = (slice(None),)
            parts.append((src.at[at], mid.at[at], dst.at[at]))
    loads = [pltpu.make_async_copy(p[0], p[1], load_sem.at[i]) for i, p in enumerate(parts)]
    puts = [pltpu.make_async_copy(p[1], p[2], store_sem.at[i]) for i, p in enumerate(parts)]
    for copy in loads:
        copy.start()
    for load, put in zip(loads, puts):
        load.wait()
        put.start()
    for copy in puts:
        copy.wait()


VM = pl.BlockSpec(memory_space=pltpu.VMEM)
SM = pl.BlockSpec(memory_space=pltpu.SMEM)
ANY = pl.BlockSpec(memory_space=pl.ANY)


def vb(*shape):
    return pltpu.VMEM(shape, BF)


def vf(*shape):
    return pltpu.VMEM(shape, F32)


def sds(shape, dtype=BF):
    return jax.ShapeDtypeStruct(shape, dtype)


def shards(block_input, modulation, iteration, positions, qkv_weight, out_weight, grad_out):
    mod = modulation.transpose(1, 0, 2)
    wq = qkv_weight.transpose(1, 0, 2)
    pos = positions.reshape(8, HALF)

    def rows(w):
        return [
            vf(4, HALF, 4 * w), vb(4, HALF, 4 * w), vb(4, HALF, 4 * w), vb(4, HALF, w),
            vb(4, 2, 96, w), vb(4, 2, HALF, w), vb(4, 2, HALF, w),
        ]

    gin, gmod, gqkv, gow = pl.pallas_call(
        kernel,
        name="block_backward",
        out_shape=(sds((96, 1024)), sds((3, 1024), F32), sds((3, 1024, 512)), sds((512, 1024))),
        in_specs=[VM, VM, VM, SM, VM, ANY, ANY],
        out_specs=(VM, VM, ANY, ANY),
        scratch_shapes=[
            vb(4, 4, 96, 1024), vb(4, 4, 96, 1024), vb(4, HALF, 256),
            vb(1024, 1536), vb(512, 1024), vb(512, 1024),
            *rows(384), *rows(128), vf(8, 128), vf(7, 8, 128), vf(8, 128), vf(7, 8, 128),
            vb(2, 4, HALF, 256), vf(4, HALF, 1536), pltpu.VMEM((4, HALF, 128), jnp.int32), vf(4, HALF, 128),
            vf(128, 1536), vf(128, 1536), vb(256, 768), vb(256, 768),
            vb(4, 2, HALF, 512), vb(4, 2, HALF, 1024), vb(4, 2, HALF, 512),
            vf(4, 384, 1024), vb(4, 4, 96, 1024),
            vb(2, 2, 96, 512), vb(2, 4, 96, 512), vb(4, 96, 512), vb(2, 48, 512), vb(2, 96, 512),
            vb(4, 2, 48, 512), vb(4, 2, 96, 512), vb(4, 96, 512), vb(2, 48, 512), vb(2, 96, 512),
            vb(1024, 1536), vb(512, 1024), vf(2, 8, 1024), vf(4, 8, 1024), vf(4, 8, 1024),
            pltpu.SemaphoreType.DMA((N_COPIES,)), pltpu.SemaphoreType.DMA((N_COPIES,)),
            pltpu.SemaphoreType.DMA((16,)), pltpu.SemaphoreType.DMA((16,)),
        ],
        compiler_params=pltpu.CompilerParams(
            collective_id=0, has_side_effects=True, vmem_limit_bytes=63 << 20
        ),
    )(block_input, grad_out, mod, iteration, pos, wq, out_weight)
    shapes = [(96, 1024), (3, 1024), (3, 1024, 512), (512, 1024)]
    types = [BF, F32, BF, BF]
    gin, gmod, gqkv, gow = pl.pallas_call(
        place_kernel,
        name="place",
        out_shape=[sds(a, b) for a, b in zip(shapes, types)],
        in_specs=[ANY] * 4,
        out_specs=[ANY] * 4,
        scratch_shapes=[pltpu.VMEM(a, b) for a, b in zip(shapes, types)]
        + [pltpu.SemaphoreType.DMA((10,)), pltpu.SemaphoreType.DMA((10,))],
        compiler_params=pltpu.CompilerParams(vmem_limit_bytes=63 << 20),
    )(gin, gmod, gqkv, gow)
    return gin, gqkv.transpose(1, 0, 2), gow, gmod


def solution(mesh):
    placed = (
        P("col", "row"),
        P(None, None, "row"),
        P(),
        P(),
        P("row", None, "col"),
        P("col", "row"),
        P("col", "row"),
    )
    return jax.shard_map(
        shards,
        mesh=mesh,
        in_specs=placed,
        out_specs=(P("col", "row"), P("row", None, "col"), P("col", "row"), P(None, "row")),
        check_vma=False,
    )
```

```python
import functools
import jax
import jax.numpy as jnp
from jax import lax
from jax.experimental import pallas as pl
from jax.experimental.pallas import tpu as pltpu
from jax.sharding import PartitionSpec as P

D = 8192
HEAD_DIM = 128
EPS = 1e-06
LOG2E = 1.4426950408889634
MESH = pl.DeviceIdType.MESH
BF = jnp.bfloat16
F32 = jnp.float32

CORE = (0, 1, 0, 0)
XP, XM, X2 = (1, 0, 0, 0), (3, 0, 0, 0), (2, 0, 0, 0)
YP, YM, Y2 = (0, 0, 1, 0), (0, 0, 3, 0), (0, 0, 2, 0)
ZP, ZM, Z2 = (0, 0, 0, 1), (0, 0, 0, 3), (0, 0, 0, 2)

G = 4
HALF = 192
F0, F1 = pl.ds(0, 512), pl.ds(512, 512)
R0, R1 = pl.ds(0, 384), pl.ds(384, 640)


def coords():
    row, col = lax.axis_index("row"), lax.axis_index("col")
    return row // 2, row % 2, col // 4, col % 4


def device(step):
    x, k, y, z = coords()
    dx, dk, dy, dz = step
    x, k, y, z = (x + dx) % 4, (k + dk) % 2, (y + dy) % 4, (z + dz) % 4
    return (x * 2 + k, y * 4 + z)


def enter(steps):
    barrier = pltpu.get_barrier_semaphore()
    for step in steps:
        pl.semaphore_signal(barrier, inc=1, device_id=device(step), device_id_type=MESH)
    pl.semaphore_wait(barrier, len(steps))


class Net:
    def __init__(self, send_sem, recv_sem):
        self.send_sem, self.recv_sem, self.copies = send_sem, recv_sem, []

    def send(self, src, dst, step):
        i = len(self.copies)
        copy = pltpu.make_async_remote_copy(
            src_ref=src,
            dst_ref=dst,
            send_sem=self.send_sem.at[i],
            recv_sem=self.recv_sem.at[i],
            device_id=device(step),
            device_id_type=MESH,
        )
        copy.start()
        self.copies.append(copy)
        return copy

    def drain(self):
        for copy in self.copies:
            copy.wait_send()


class Line:
    def __init__(self, net, at, up, down, rows):
        self.net, self.at, self.up, self.down, self.half = net, at, up, down, rows // 2
        self.all = pl.ds(0, rows)

    def put(self, step, rows, way):
        ref = self.at(step, rows)
        return self.net.send(ref, ref, way)

    def start(self):
        self.a, self.b = self.put(0, self.all, self.up), self.put(0, self.all, self.down)

    def forward_up(self):
        self.a.wait_recv()
        self.c = self.put(3, pl.ds(0, self.half), self.up)

    def forward_down(self):
        self.b.wait_recv()
        self.d = self.put(1, pl.ds(self.half, self.half), self.down)

    def forward(self):
        self.forward_up()
        self.forward_down()

    def end(self):
        self.c.wait_recv()
        self.d.wait_recv()


class Gather:
    def __init__(self, net, buf):
        _, _, y, z = coords()

        def along_y(zz, cols):
            return Line(net, lambda n, rows: buf.at[(y + n) % 4, zz, rows, cols], YP, YM, 96)

        def along_z(yy, cols):
            return Line(net, lambda n, rows: buf.at[yy, (z + n) % 4, rows, cols], ZP, ZM, 96)

        self.a, self.b = along_y(z, F0), along_z(y, F1)
        self.zs = [along_z((y + n) % 4, F0) for n in range(4)]
        self.ys = [along_y((z + n) % 4, F1) for n in range(4)]

    def s1(self):
        for line in (self.a, self.b, self.zs[0], self.ys[0]):
            line.start()

    def s2(self):
        self.a.forward_up()
        self.zs[3].start()
        self.b.forward_up()
        self.ys[3].start()
        self.a.forward_down()
        self.zs[1].start()
        self.b.forward_down()
        self.ys[1].start()

    def s3(self):
        self.zs[0].forward()
        self.ys[0].forward()
        self.a.end()
        self.zs[2].start()
        self.b.end()
        self.ys[2].start()
        self.zs[0].end()

    def s4(self):
        for n in (3, 1):
            self.zs[n].forward()
            self.ys[n].forward()

    def s5(self):
        self.zs[2].forward()
        self.ys[2].forward()
        self.zs[3].end()
        self.zs[1].end()

    def s6(self):
        self.zs[2].end()
        for line in self.ys:
            line.end()


class RowReduce:
    def __init__(self, net, own, part, sib, hop, hop_in, out_buf, in_buf, w):
        self.net, self.own, self.part, self.sib = net, own, part, sib
        self.hop, self.hop_in, self.out_buf, self.in_buf, self.w = hop, hop_in, out_buf, in_buf, w
        self.c, self.h, self.f = {}, {}, {}

    def start(self, s):
        self.c[s] = self.net.send(self.part.at[s], self.sib.at[s], CORE)

    def local(self, s, d, rows):
        cols = pl.ds(d * self.w, self.w)
        return self.own[s, rows, cols] + self.sib[s, rows, cols].astype(F32)

    def put(self, s, i, rows, way):
        copy = self.net.send(self.out_buf.at[s, i, rows], self.in_buf.at[s, i, rows], way)
        self.f.setdefault(s, []).append(copy)

    def r1(self, s):
        lo, hi = pl.ds(0, 96), pl.ds(96, 96)
        self.c[s].wait_recv()
        self.hop[s] = self.local(s, 0, pl.ds(0, HALF)).astype(BF)
        self.h[s] = (
            self.net.send(self.hop.at[s, lo], self.hop_in.at[s, 0], XP),
            self.net.send(self.hop.at[s, hi], self.hop_in.at[s, 1], XM),
        )
        self.out_buf[s, 0, hi] = self.local(s, 1, hi).astype(BF)
        self.put(s, 0, hi, XP)
        self.out_buf[s, 1, lo] = self.local(s, 2, lo).astype(BF)
        self.put(s, 1, lo, XM)

    def r2(self, s):
        a, b = self.h[s]
        lo, hi = pl.ds(0, 96), pl.ds(96, 96)
        a.wait_recv()
        self.out_buf[s, 0, lo] = (self.local(s, 1, lo) + self.hop_in[s, 0].astype(F32)).astype(BF)
        self.put(s, 0, lo, XP)
        b.wait_recv()
        self.out_buf[s, 1, hi] = (self.local(s, 2, hi) + self.hop_in[s, 1].astype(F32)).astype(BF)
        self.put(s, 1, hi, XM)

    def r3(self, s):
        own = self.local(s, 3, pl.ds(0, HALF))
        for copy in self.f[s]:
            copy.wait_recv()
        return (own + self.in_buf[s, 0].astype(F32) + self.in_buf[s, 1].astype(F32)).astype(BF)


OTHERS = [(dx, dk, 0, 0) for dx in range(4) for dk in range(2) if (dx, dk) != (0, 0)]


class RowSum:
    def __init__(self, net, mine, got, value):
        self.mine, self.got = mine, got
        wide = jnp.concatenate([jnp.broadcast_to(value, (96, 128)), jnp.zeros((32, 128), F32)], axis=0)
        mine[...] = wide.T[0:8]
        self.copies = [net.send(mine, got.at[i], step) for i, step in enumerate(OTHERS)]

    def total(self):
        for copy in self.copies:
            copy.wait_recv()
        total = self.mine[...]
        for i in range(7):
            total += self.got[i]
        return jnp.broadcast_to(total[0:1], (128, 128)).T[0:96, 0:1]


def heads_of(x):
    return ((x + 2) % 4, (x + 1) % 4, (x + 3) % 4, x)


def load_weights(wq_hbm, wo_hbm, wv, wo, sem):
    x, _, _, _ = coords()
    copies = []
    for d, head in enumerate(heads_of(x)):
        cols = pl.ds(pl.multiple_of(head * 128, 128), 128)
        for j, place in enumerate((d * 128, 512 + d * 256, 640 + d * 256)):
            copies.append((wq_hbm.at[j, :, cols], wv.at[:, pl.ds(place, 128)]))
        copies.append((wo_hbm.at[cols, :], wo.at[pl.ds(d * 128, 128)]))
    copies = [pltpu.make_async_copy(a, b, sem.at[i]) for i, (a, b) in enumerate(copies)]
    for copy in copies:
        copy.start()
    return copies


class RowGather:
    def __init__(self, net, at, w):
        self.net, self.at, self.w = net, at, w

    def cols(self, d, n=1):
        return pl.ds(d * self.w, n * self.w)

    def start(self):
        own = self.at(slice(None), self.cols(3))
        self.up = self.net.send(own, self.at(slice(None), self.cols(2)), XP)
        self.down = self.net.send(own, self.at(slice(None), self.cols(1)), XM)

    def forward(self):
        lo, hi = pl.ds(0, 96), pl.ds(96, 96)
        self.up.wait_recv()
        self.up2 = self.net.send(self.at(lo, self.cols(2)), self.at(lo, self.cols(0)), XP)
        self.down.wait_recv()
        self.down2 = self.net.send(self.at(hi, self.cols(1)), self.at(hi, self.cols(0)), XM)
        near = self.at(slice(None), self.cols(1, 3))
        self.near = self.net.send(near, near, CORE)

    def finish(self):
        self.up2.wait_recv()
        self.down2.wait_recv()
        far = self.at(slice(None), self.cols(0))
        self.far = self.net.send(far, far, CORE)

    def end(self):
        self.near.wait_recv()
        self.far.wait_recv()


class RingReduce:
    def __init__(self, net, up, down, hop_in, last_in, lo, hi):
        self.net, self.up, self.down, self.hop_in, self.last_in = net, up, down, hop_in, last_in
        self.lo, self.hi, self.tail = lo, hi, []

    def far(self, chunk):
        self.a = self.net.send(chunk.at[self.lo], self.hop_in.at[0], self.up)
        self.b = self.net.send(chunk.at[self.hi], self.hop_in.at[1], self.down)

    def put(self, chunk, i, rows, way):
        self.tail.append(self.net.send(chunk.at[rows], self.last_in.at[i].at[rows], way))

    def above_now(self, chunk):
        self.put(chunk, 0, self.hi, self.up)

    def below_now(self, chunk):
        self.put(chunk, 1, self.lo, self.down)

    def above(self, chunk):
        part = chunk.at[self.lo]
        self.a.wait_recv()
        part[...] = (part[...].astype(F32) + self.hop_in[0].astype(F32)).astype(BF)
        self.put(chunk, 0, self.lo, self.up)

    def below(self, chunk):
        part = chunk.at[self.hi]
        self.b.wait_recv()
        part[...] = (part[...].astype(F32) + self.hop_in[1].astype(F32)).astype(BF)
        self.put(chunk, 1, self.hi, self.down)

    def last(self, own):
        own = own.astype(F32)
        for copy in self.tail:
            copy.wait_recv()
        return own + self.last_in[0].astype(F32) + self.last_in[1].astype(F32)


NT = (((1,), (1,)), ((), ()))
TN = (((0,), (0,)), ((), ()))
N_COPIES = 40 * 2 + 7 * 4 * 2 + 14 + 4 + 6 * 9 + 1 + 42 + 6


def kernel(
    x_ref, gout_ref, mod_ref, it_ref, pos_ref, wq_hbm, wo_hbm,
    gin, gmod, gqkv, gow,
    nf, gf, qkvg, wv, wo, wog,
    aq, pq, rq, hq, hqi, oq, iq, ag, pg, rg, hg, hgi, og, ig, mine, got, mine2, got2,
    kv, wts, pos_t, stats, dk, dv, part, part_in,
    gpq, gpkv, cx, gnq, gn, yh0, yi0, t0, zh0, zi0, zh1, zi1, t1, yh1, yi1,
    outq, ow, sums, sums_z, sums_y,
    send_sem, recv_sem, load_sem, store_sem,
):
    x, k, y, z = coords()
    net = Net(send_sem, recv_sem)
    loads = load_weights(wq_hbm, wo_hbm, wv, wo, load_sem)
    enter(OTHERS + [YP, YM, Y2, ZP, ZM, Z2])
    it = it_ref[0]
    shift, scale, gate = [mod_ref[i, pl.ds(it, 1), :] for i in range(3)]

    gf[y, z] = gout_ref[...]
    cot = Gather(net, gf)
    cot.s1()
    xf = x_ref[...].astype(F32)
    squares = RowSum(net, mine, got, jnp.sum(xf * xf, axis=1, keepdims=True))
    pos = [[pos_ref[:, pl.ds(g * 384 + h * HALF, HALF)] for g in range(4)] for h in range(2)]
    key_pos = jnp.concatenate(pos[0] + pos[1], axis=1)
    for g in range(4):
        own_pos = jnp.where(k == 0, pos[0][g], pos[1][g])
        pos_t[g] = jnp.broadcast_to(own_pos, (128, HALF)).T
    inv = lax.rsqrt(squares.total() / D + EPS)
    nf[y, z] = (xf * inv * (1.0 + scale) + shift).astype(BF)
    act = Gather(net, nf)
    act.s1()
    order = (y, (y + 3) % 4, (y + 1) % 4, (y + 2) % 4)
    rows_q = RowReduce(net, aq, pq, rq, hq, hqi, oq, iq, 384)
    rows_g = RowReduce(net, ag, pg, rg, hg, hgi, og, ig, 128)

    def half_of(buf, s, h):
        return buf[order[s], pl.ds(2 * h, 2)].reshape(HALF, 1024)

    def multiply(s):
        for h, dst in ((1 - k, pq), (k, aq)):
            a = half_of(nf, s, h)
            r = jnp.dot(a, wv[:, pl.ds(0, 512)], preferred_element_type=F32).astype(dst.dtype)
            for d in range(4):
                dst[s, :, pl.ds(d * 384, 128)] = r[:, d * 128 : d * 128 + 128]
            r = jnp.dot(a, wv[:, pl.ds(512, 1024)], preferred_element_type=F32).astype(dst.dtype)
            for d in range(4):
                dst[s, :, pl.ds(d * 384 + 128, 256)] = r[:, d * 256 : d * 256 + 256]
            if dst is pq:
                rows_q.start(s)

    def multiply_g(s):
        for h, dst in ((1 - k, pg), (k, ag)):
            r = lax.dot_general(half_of(gf, s, h), wog[...], NT, preferred_element_type=F32)
            dst[s] = r.astype(dst.dtype)
            if dst is pg:
                rows_g.start(s)

    swaps = []

    def finish(s):
        r = rows_q.r3(s)
        qkvg[order[s], :, pl.ds(0, 128)] = r[:, 0:128]
        kv[k, order[s]] = r[:, 128:384]
        half = kv.at[k, order[s]]
        swaps.append(net.send(half, half, CORE))

    def finish_g(s):
        qkvg[order[s], :, pl.ds(128, 128)] = rows_g.r3(s)

    act.s2()
    for copy in loads:
        copy.wait()
    act.s3()
    multiply(0)
    act.s4()
    cot.s2()
    rows_q.r1(0)
    act.s5()
    multiply(1)
    cot.s3()
    rows_q.r2(0)
    multiply(2)
    rows_q.r1(1)
    act.s6()
    cot.s4()
    multiply(3)
    rows_q.r1(2)
    rows_q.r2(1)
    wog[...] = (wo[...].astype(F32) * gate).astype(BF)
    rows_q.r1(3)
    cot.s5()
    rows_q.r2(2)
    multiply_g(0)
    multiply_g(1)
    finish(0)
    rows_q.r2(3)
    rows_g.r1(0)
    multiply_g(2)
    rows_g.r1(1)
    finish(1)
    cot.s6()
    multiply_g(3)
    finish(2)
    rows_g.r1(2)
    rows_g.r2(0)
    finish(3)
    rows_g.r1(3)
    rows_g.r2(1)

    groups = ((y + 2) % 4, (y + 1) % 4, (y + 3) % 4, y)
    for copy in swaps:
        copy.wait_recv()
    keys = kv[:, :, :, pl.ds(0, 128)].reshape(1536, 128)
    values = kv[:, :, :, pl.ds(128, 128)].reshape(1536, 128)
    factor = 1.0 / HEAD_DIM**0.5

    def attend(s):
        q = qkvg[groups[s], :, pl.ds(0, 128)]
        scores = lax.dot_general(q, keys, NT, preferred_element_type=F32)
        scores = jnp.where(key_pos <= pos_t[groups[s], :, pl.ds(0, 1)], scores, -1e30)
        peak = jnp.max(scores, axis=1, keepdims=True)
        weights = jnp.exp2((scores - peak) * (factor * LOG2E))
        wts[s] = weights
        inverse = 1.0 / jnp.sum(weights, axis=1, keepdims=True)
        stats[s] = jnp.broadcast_to(inverse, (HALF, 128))
        probs_b = (weights * inverse).astype(BF)
        r = jnp.dot(probs_b, values, preferred_element_type=F32)
        cx[groups[s], k, :, pl.ds(384, 128)] = r.astype(BF)

    def attend_grad(s):
        q = qkvg[groups[s], :, pl.ds(0, 128)]
        g = qkvg[groups[s], :, pl.ds(128, 128)]
        weights, inverse = wts[s], stats[s, :, pl.ds(0, 1)]
        probs_b = (weights * inverse).astype(BF)
        grad_probs = lax.dot_general(g, values, NT, preferred_element_type=F32)
        delta = jnp.sum(weights * grad_probs, axis=1, keepdims=True) * inverse
        grad_scores = (weights * (grad_probs - delta) * (inverse * factor)).astype(BF)
        r = jnp.dot(grad_scores, keys, preferred_element_type=F32)
        gpq[groups[s], k, :, pl.ds(384, 128)] = r.astype(BF)
        grad_k = jnp.dot(q.T, grad_scores, preferred_element_type=F32)
        grad_v = jnp.dot(g.T, probs_b, preferred_element_type=F32)
        if s == 3:
            dk[...] = grad_k
            dv[...] = grad_v
        else:
            dk[...] += grad_k
            dv[...] += grad_v

    def gather_q(s):
        return RowGather(net, lambda rows, cols: gpq.at[groups[s], k, rows, cols], 128)

    def gather_kv(s):
        return RowGather(net, lambda rows, cols: gpkv.at[groups[s], k, rows, cols], 256)

    moves_q = [gather_q(s) for s in range(4)]
    moves_kv = [gather_kv(s) for s in range(4)]
    context = RowGather(net, lambda rows, cols: cx.at[:, k, rows, cols], 128)

    attend(0)
    rows_g.r2(2)
    attend(1)
    attend(2)
    rows_g.r2(3)
    attend(3)
    for i in range(4):
        finish_g(i)
        attend_grad(3 - i)
        if i < 3:
            moves_q[3 - i].start()
    mine_at = pl.ds(pl.multiple_of(k * 768, 128), 768)
    theirs_at = pl.ds(pl.multiple_of((1 - k) * 768, 128), 768)
    part[pl.ds(0, 128)] = dk[:, theirs_at].astype(BF)
    part[pl.ds(128, 128)] = dv[:, theirs_at].astype(BF)
    swap = net.send(part, part_in, CORE)
    moves_q[0].start()

    stores = []

    def store(src, dst):
        copy = pltpu.make_async_copy(src, dst, store_sem.at[len(stores)])
        copy.start()
        stores.append(copy)

    heads = heads_of(x)
    head_at = [pl.ds(pl.multiple_of(head * 128, 128), 128) for head in heads]
    lo, hi = pl.ds(0, 48), pl.ds(48, 48)
    ring_y0 = RingReduce(net, YP, YM, yh0, yi0, pl.ds(0, 2), pl.ds(2, 2))
    rings_z1 = [RingReduce(net, ZP, ZM, zh1.at[s], zi1.at[s], lo, hi) for s in range(4)]
    ring_z0 = RingReduce(net, ZP, ZM, zh0, zi0, lo, hi)
    ring_y1 = RingReduce(net, YP, YM, yh1, yi1, lo, hi)
    zp, zm, z2 = (z + 1) % 4, (z + 3) % 4, (z + 2) % 4

    def normed_q(s):
        moves_q[s].end()
        a = gpq[groups[s]].reshape(384, 512)
        gnq[s] = lax.dot_general(a, wv[:, pl.ds(0, 512)], NT, preferred_element_type=F32)

    def normed_kv(s):
        moves_kv[s].end()
        a = gpkv[groups[s]].reshape(384, 1024)
        r = lax.dot_general(a, wv[:, pl.ds(512, 1024)], NT, preferred_element_type=F32)
        gn[s] = (gnq[s] + r).astype(BF).reshape(4, 96, 1024)

    def out_weight():
        context.end()
        all_g = gf[...].reshape(1536, 1024)
        gate_grad = jnp.zeros((1, 1024), F32)
        for m in range(2):
            rows = pl.ds(m * 256, 256)
            left = cx[:, :, :, rows].reshape(1536, 256)
            r = lax.dot_general(left, all_g, TN, preferred_element_type=F32)
            gate_grad += jnp.sum(r * wo[rows, :].astype(F32), axis=0, keepdims=True)
            ow[rows, :] = (r * gate).astype(BF)
        for d in range(4):
            store(ow.at[pl.ds(d * 128, 128)], gow.at[head_at[d], :])
        return gate_grad

    def weight_q(m):
        rows = pl.ds(m * 256, 256)
        left = nf[:, :, :, rows].reshape(1536, 256)
        right = gpq[...].reshape(1536, 512)
        r = lax.dot_general(left, right, TN, preferred_element_type=F32)
        outq[rows, pl.ds(0, 512)] = r.astype(BF)

    def weight_kv(m):
        rows = pl.ds(m * 256, 256)
        left = nf[:, :, :, rows].reshape(1536, 256)
        right = gpkv[...].reshape(1536, 1024)
        r = lax.dot_general(left, right, TN, preferred_element_type=F32)
        outq[rows, pl.ds(512, 1024)] = r.astype(BF)

    def z1_far(s):
        rings_z1[s].far(gn.at[s, z2, :, R1])
        rings_z1[s].above_now(gn.at[s, zp, :, R1])
        rings_z1[s].below_now(gn.at[s, zm, :, R1])

    def z1_near(s):
        rings_z1[s].above(gn.at[s, zp, :, R1])
        rings_z1[s].below(gn.at[s, zm, :, R1])

    def z1_last(s):
        return rings_z1[s].last(gn[s, z, :, R1])

    def rows_of(s):
        return gn.at[s, :, :, R0]

    swap.wait_recv()
    for i, total in ((0, dk), (1, dv)):
        r = total[:, mine_at] + part_in[pl.ds(i * 128, 128)].astype(F32)
        gpkv[:, k, :, pl.ds(768 + i * 128, 128)] = r.T.astype(BF).reshape(4, HALF, 128)
    moves_kv[0].start()
    moves_kv[1].start()
    for s in (3, 2, 1, 0):
        moves_q[s].forward()
    moves_kv[0].forward()
    moves_kv[2].start()
    for s in (3, 2, 1, 0):
        moves_q[s].finish()
    moves_kv[1].forward()
    moves_kv[3].start()
    normed_q(0)
    normed_q(1)
    moves_kv[0].finish()
    normed_q(2)
    normed_q(3)
    normed_kv(0)
    ring_y0.far(rows_of(0))
    z1_far(0)
    moves_kv[2].forward()
    moves_kv[1].finish()
    weight_q(0)
    weight_q(1)
    normed_kv(1)
    ring_y0.above_now(rows_of(1))
    z1_far(1)
    moves_kv[3].forward()
    context.start()
    moves_kv[2].finish()
    z1_near(0)
    weight_q(2)
    normed_kv(2)
    ring_y0.below_now(rows_of(2))
    z1_far(2)
    moves_kv[3].finish()
    ring_y0.above(rows_of(1))
    z1_near(1)
    normed_kv(3)
    z1_far(3)
    ring_y0.below(rows_of(2))
    t1[0] = z1_last(0).astype(BF)
    ring_y1.far(t1.at[0])
    z1_near(2)
    context.forward()
    t1[1] = z1_last(1).astype(BF)
    ring_y1.above_now(t1.at[1])
    weight_q(3)
    z1_near(3)
    t0[...] = ring_y0.last(gn[3, :, :, R0]).astype(BF)
    ring_z0.far(t0.at[z2])
    ring_z0.above_now(t0.at[zp])
    ring_z0.below_now(t0.at[zm])
    ring_y1.above(t1.at[1])
    t1[2] = z1_last(2).astype(BF)
    ring_y1.below_now(t1.at[2])
    ring_y1.below(t1.at[2])
    context.finish()
    weight_kv(0)
    weight_kv(1)
    ring_z0.above(t0.at[zp])
    ring_z0.below(t0.at[zm])
    gate_grad = out_weight()
    t1[3] = z1_last(3).astype(BF)

    grad0 = ring_z0.last(t0[z])
    grad1 = ring_y1.last(t1[3])
    grad = jnp.concatenate([grad0, grad1], axis=1)
    x_hat = x_ref[...].astype(F32) * inv
    grad_hat = grad * (1.0 + scale)
    sums[0, pl.ds(0, 1)] = jnp.sum(grad, axis=0, keepdims=True)
    sums[0, pl.ds(1, 1)] = jnp.sum(grad * x_hat, axis=0, keepdims=True)
    sums[0, pl.ds(2, 1)] = gate_grad
    sums[0, pl.ds(3, 5)] = jnp.zeros((5, 1024), F32)
    sums_z[z] = sums[0]
    zc = [net.send(sums.at[0], sums_z.at[z], step) for step in (ZP, ZM, Z2)]
    inner = RowSum(net, mine2, got2, jnp.sum(grad_hat * x_hat, axis=1, keepdims=True))
    weight_kv(2)
    weight_kv(3)
    for d in range(4):
        for j, place in enumerate((d * 128, 512 + d * 256, 640 + d * 256)):
            store(outq.at[:, pl.ds(place, 128)], gqkv.at[j, :, head_at[d]])
    for copy in zc:
        copy.wait_recv()
    sums[1] = (sums_z[0] + sums_z[1]) + (sums_z[2] + sums_z[3])
    sums_y[y] = sums[1]
    yc = [net.send(sums.at[1], sums_y.at[y], step) for step in (YP, YM, Y2)]
    inner = inner.total() / D
    gin[...] = ((grad_hat - x_hat * inner) * inv + gout_ref[...].astype(F32)).astype(BF)
    for copy in yc:
        copy.wait_recv()
    gmod[...] = ((sums_y[0] + sums_y[1]) + (sums_y[2] + sums_y[3]))[0:3]
    net.drain()
    for copy in stores:
        copy.wait()


def place_kernel(a, b, c, d, oa, ob, oc, od, va, vb_, vc, vd, load_sem, store_sem):
    parts = []
    for src, mid, dst, n in ((a, va, oa, 1), (b, vb_, ob, 1), (c, vc, oc, 6), (d, vd, od, 2)):
        for i in range(n):
            if n == 6:
                at = (i // 2, pl.ds(512 * (i % 2), 512))
            elif n == 2:
                at = (pl.ds(256 * i, 256),)
            else:
                at = (slice(None),)
            parts.append((src.at[at], mid.at[at], dst.at[at]))
    loads = [pltpu.make_async_copy(p[0], p[1], load_sem.at[i]) for i, p in enumerate(parts)]
    puts = [pltpu.make_async_copy(p[1], p[2], store_sem.at[i]) for i, p in enumerate(parts)]
    for copy in loads:
        copy.start()
    for load, put in zip(loads, puts):
        load.wait()
        put.start()
    for copy in puts:
        copy.wait()


VM = pl.BlockSpec(memory_space=pltpu.VMEM)
SM = pl.BlockSpec(memory_space=pltpu.SMEM)
ANY = pl.BlockSpec(memory_space=pl.ANY)


def vb(*shape):
    return pltpu.VMEM(shape, BF)


def vf(*shape):
    return pltpu.VMEM(shape, F32)


def sds(shape, dtype=BF):
    return jax.ShapeDtypeStruct(shape, dtype)


def shards(block_input, modulation, iteration, positions, qkv_weight, out_weight, grad_out):
    mod = modulation.transpose(1, 0, 2)
    wq = qkv_weight.transpose(1, 0, 2)
    pos = positions.reshape(1, 1536)

    def rows(w):
        return [
            vf(4, HALF, 4 * w), vb(4, HALF, 4 * w), vb(4, HALF, 4 * w), vb(4, HALF, w),
            vb(4, 2, 96, w), vb(4, 2, HALF, w), vb(4, 2, HALF, w),
        ]

    gin, gmod, gqkv, gow = pl.pallas_call(
        kernel,
        name="block_backward",
        out_shape=(sds((96, 1024)), sds((3, 1024), F32), sds((3, 1024, 512)), sds((512, 1024))),
        in_specs=[VM, VM, VM, SM, VM, ANY, ANY],
        out_specs=(VM, VM, ANY, ANY),
        scratch_shapes=[
            vb(4, 4, 96, 1024), vb(4, 4, 96, 1024), vb(4, HALF, 256),
            vb(1024, 1536), vb(512, 1024), vb(512, 1024),
            *rows(384), *rows(128), vf(8, 128), vf(7, 8, 128), vf(8, 128), vf(7, 8, 128),
            vb(2, 4, HALF, 256), vf(4, HALF, 1536), pltpu.VMEM((4, HALF, 128), jnp.int32), vf(4, HALF, 128),
            vf(128, 1536), vf(128, 1536), vb(256, 768), vb(256, 768),
            vb(4, 2, HALF, 512), vb(4, 2, HALF, 1024), vb(4, 2, HALF, 512),
            vf(4, 384, 1024), vb(4, 4, 96, 1024),
            vb(2, 2, 96, 384), vb(2, 4, 96, 384), vb(4, 96, 384), vb(2, 48, 384), vb(2, 96, 384),
            vb(4, 2, 48, 640), vb(4, 2, 96, 640), vb(4, 96, 640), vb(2, 48, 640), vb(2, 96, 640),
            vb(1024, 1536), vb(512, 1024), vf(2, 8, 1024), vf(4, 8, 1024), vf(4, 8, 1024),
            pltpu.SemaphoreType.DMA((N_COPIES,)), pltpu.SemaphoreType.DMA((N_COPIES,)),
            pltpu.SemaphoreType.DMA((16,)), pltpu.SemaphoreType.DMA((16,)),
        ],
        compiler_params=pltpu.CompilerParams(
            collective_id=0, has_side_effects=True, vmem_limit_bytes=63 << 20
        ),
    )(block_input, grad_out, mod, iteration, pos, wq, out_weight)
    shapes = [(96, 1024), (3, 1024), (3, 1024, 512), (512, 1024)]
    types = [BF, F32, BF, BF]
    gin, gmod, gqkv, gow = pl.pallas_call(
        place_kernel,
        name="place",
        out_shape=[sds(a, b) for a, b in zip(shapes, types)],
        in_specs=[ANY] * 4,
        out_specs=[ANY] * 4,
        scratch_shapes=[pltpu.VMEM(a, b) for a, b in zip(shapes, types)]
        + [pltpu.SemaphoreType.DMA((10,)), pltpu.SemaphoreType.DMA((10,))],
        compiler_params=pltpu.CompilerParams(vmem_limit_bytes=63 << 20),
    )(gin, gmod, gqkv, gow)
    return gin, gqkv.transpose(1, 0, 2), gow, gmod


def solution(mesh):
    placed = (
        P("col", "row"),
        P(None, None, "row"),
        P(),
        P(),
        P("row", None, "col"),
        P("col", "row"),
        P("col", "row"),
    )
    return jax.shard_map(
        shards,
        mesh=mesh,
        in_specs=placed,
        out_specs=(P("col", "row"), P("row", None, "col"), P("col", "row"), P(None, "row")),
        check_vma=False,
    )
```

```python
import functools
import jax
import jax.numpy as jnp
from jax import lax
from jax.experimental import pallas as pl
from jax.experimental.pallas import tpu as pltpu
from jax.sharding import PartitionSpec as P

D = 8192
HEAD_DIM = 128
EPS = 1e-06
LOG2E = 1.4426950408889634
MESH = pl.DeviceIdType.MESH
BF = jnp.bfloat16
F32 = jnp.float32

CORE = (0, 1, 0, 0)
XP, XM, X2 = (1, 0, 0, 0), (3, 0, 0, 0), (2, 0, 0, 0)
YP, YM, Y2 = (0, 0, 1, 0), (0, 0, 3, 0), (0, 0, 2, 0)
ZP, ZM, Z2 = (0, 0, 0, 1), (0, 0, 0, 3), (0, 0, 0, 2)

G = 4
HALF = 192
F0, F1 = pl.ds(0, 512), pl.ds(512, 512)
R0, R1 = pl.ds(0, 384), pl.ds(384, 640)


def coords():
    row, col = lax.axis_index("row"), lax.axis_index("col")
    return row // 2, row % 2, col // 4, col % 4


def device(step):
    x, k, y, z = coords()
    dx, dk, dy, dz = step
    x, k, y, z = (x + dx) % 4, (k + dk) % 2, (y + dy) % 4, (z + dz) % 4
    return (x * 2 + k, y * 4 + z)


def enter(steps):
    barrier = pltpu.get_barrier_semaphore()
    for step in steps:
        pl.semaphore_signal(barrier, inc=1, device_id=device(step), device_id_type=MESH)
    pl.semaphore_wait(barrier, len(steps))


class Net:
    def __init__(self, send_sem, recv_sem):
        self.send_sem, self.recv_sem, self.copies = send_sem, recv_sem, []

    def send(self, src, dst, step):
        i = len(self.copies)
        copy = pltpu.make_async_remote_copy(
            src_ref=src,
            dst_ref=dst,
            send_sem=self.send_sem.at[i],
            recv_sem=self.recv_sem.at[i],
            device_id=device(step),
            device_id_type=MESH,
        )
        copy.start()
        self.copies.append(copy)
        return copy

    def drain(self):
        for copy in self.copies:
            copy.wait_send()


class Line:
    def __init__(self, net, at, up, down, rows):
        self.net, self.at, self.up, self.down, self.half = net, at, up, down, rows // 2
        self.all = pl.ds(0, rows)

    def put(self, step, rows, way):
        ref = self.at(step, rows)
        return self.net.send(ref, ref, way)

    def start(self):
        self.a, self.b = self.put(0, self.all, self.up), self.put(0, self.all, self.down)

    def forward_up(self):
        self.a.wait_recv()
        self.c = self.put(3, pl.ds(0, self.half), self.up)

    def forward_down(self):
        self.b.wait_recv()
        self.d = self.put(1, pl.ds(self.half, self.half), self.down)

    def forward(self):
        self.forward_up()
        self.forward_down()

    def end(self):
        self.c.wait_recv()
        self.d.wait_recv()


class Gather:
    def __init__(self, net, buf):
        _, _, y, z = coords()

        def along_y(zz, cols):
            return Line(net, lambda n, rows: buf.at[(y + n) % 4, zz, rows, cols], YP, YM, 96)

        def along_z(yy, cols):
            return Line(net, lambda n, rows: buf.at[yy, (z + n) % 4, rows, cols], ZP, ZM, 96)

        self.a, self.b = along_y(z, F0), along_z(y, F1)
        self.zs = [along_z((y + n) % 4, F0) for n in range(4)]
        self.ys = [along_y((z + n) % 4, F1) for n in range(4)]

    def s1(self):
        for line in (self.a, self.b, self.zs[0], self.ys[0]):
            line.start()

    def s2(self):
        self.a.forward_up()
        self.zs[3].start()
        self.b.forward_up()
        self.ys[3].start()
        self.a.forward_down()
        self.zs[1].start()
        self.b.forward_down()
        self.ys[1].start()

    def s3(self):
        self.zs[0].forward()
        self.ys[0].forward()
        self.a.end()
        self.zs[2].start()
        self.b.end()
        self.ys[2].start()
        self.zs[0].end()

    def s4(self):
        for n in (3, 1):
            self.zs[n].forward()
            self.ys[n].forward()

    def s5(self):
        self.zs[2].forward()
        self.ys[2].forward()
        self.zs[3].end()
        self.zs[1].end()

    def s6(self):
        self.zs[2].end()
        for line in self.ys:
            line.end()


class RowReduce:
    def __init__(self, net, own, part, sib, hop, hop_in, out_buf, in_buf, w):
        self.net, self.own, self.part, self.sib = net, own, part, sib
        self.hop, self.hop_in, self.out_buf, self.in_buf, self.w = hop, hop_in, out_buf, in_buf, w
        self.c, self.h, self.f = {}, {}, {}

    def start(self, s):
        self.c[s] = self.net.send(self.part.at[s], self.sib.at[s], CORE)

    def local(self, s, d, rows):
        cols = pl.ds(d * self.w, self.w)
        return self.own[s, rows, cols] + self.sib[s, rows, cols].astype(F32)

    def put(self, s, i, rows, way):
        copy = self.net.send(self.out_buf.at[s, i, rows], self.in_buf.at[s, i, rows], way)
        self.f.setdefault(s, []).append(copy)

    def r1(self, s):
        lo, hi = pl.ds(0, 96), pl.ds(96, 96)
        self.c[s].wait_recv()
        self.hop[s] = self.local(s, 0, pl.ds(0, HALF)).astype(BF)
        self.h[s] = (
            self.net.send(self.hop.at[s, lo], self.hop_in.at[s, 0], XP),
            self.net.send(self.hop.at[s, hi], self.hop_in.at[s, 1], XM),
        )
        self.out_buf[s, 0, hi] = self.local(s, 1, hi).astype(BF)
        self.put(s, 0, hi, XP)
        self.out_buf[s, 1, lo] = self.local(s, 2, lo).astype(BF)
        self.put(s, 1, lo, XM)

    def r2(self, s):
        a, b = self.h[s]
        lo, hi = pl.ds(0, 96), pl.ds(96, 96)
        a.wait_recv()
        self.out_buf[s, 0, lo] = (self.local(s, 1, lo) + self.hop_in[s, 0].astype(F32)).astype(BF)
        self.put(s, 0, lo, XP)
        b.wait_recv()
        self.out_buf[s, 1, hi] = (self.local(s, 2, hi) + self.hop_in[s, 1].astype(F32)).astype(BF)
        self.put(s, 1, hi, XM)

    def r3(self, s):
        own = self.local(s, 3, pl.ds(0, HALF))
        for copy in self.f[s]:
            copy.wait_recv()
        return (own + self.in_buf[s, 0].astype(F32) + self.in_buf[s, 1].astype(F32)).astype(BF)


OTHERS = [(dx, dk, 0, 0) for dx in range(4) for dk in range(2) if (dx, dk) != (0, 0)]


class RowSum:
    def __init__(self, net, mine, got, value):
        self.mine, self.got = mine, got
        wide = jnp.concatenate([jnp.broadcast_to(value, (96, 128)), jnp.zeros((32, 128), F32)], axis=0)
        mine[...] = wide.T[0:8]
        self.copies = [net.send(mine, got.at[i], step) for i, step in enumerate(OTHERS)]

    def total(self):
        for copy in self.copies:
            copy.wait_recv()
        total = self.mine[...]
        for i in range(7):
            total += self.got[i]
        return jnp.broadcast_to(total[0:1], (128, 128)).T[0:96, 0:1]


def heads_of(x):
    return ((x + 2) % 4, (x + 1) % 4, (x + 3) % 4, x)


def load_weights(wq_hbm, wo_hbm, wv, wo, sem):
    x, _, _, _ = coords()
    copies = []
    for d, head in enumerate(heads_of(x)):
        cols = pl.ds(pl.multiple_of(head * 128, 128), 128)
        for j, place in enumerate((d * 128, 512 + d * 256, 640 + d * 256)):
            copies.append((wq_hbm.at[j, :, cols], wv.at[:, pl.ds(place, 128)]))
        copies.append((wo_hbm.at[cols, :], wo.at[pl.ds(d * 128, 128)]))
    copies = [pltpu.make_async_copy(a, b, sem.at[i]) for i, (a, b) in enumerate(copies)]
    for copy in copies:
        copy.start()
    return copies


class RowGather:
    def __init__(self, net, at, w):
        self.net, self.at, self.w = net, at, w

    def cols(self, d, n=1):
        return pl.ds(d * self.w, n * self.w)

    def start(self):
        own = self.at(slice(None), self.cols(3))
        self.up = self.net.send(own, self.at(slice(None), self.cols(2)), XP)
        self.down = self.net.send(own, self.at(slice(None), self.cols(1)), XM)

    def forward(self):
        lo, hi = pl.ds(0, 96), pl.ds(96, 96)
        self.up.wait_recv()
        self.up2 = self.net.send(self.at(lo, self.cols(2)), self.at(lo, self.cols(0)), XP)
        self.down.wait_recv()
        self.down2 = self.net.send(self.at(hi, self.cols(1)), self.at(hi, self.cols(0)), XM)
        near = self.at(slice(None), self.cols(1, 3))
        self.near = self.net.send(near, near, CORE)

    def finish(self):
        self.up2.wait_recv()
        self.down2.wait_recv()
        far = self.at(slice(None), self.cols(0))
        self.far = self.net.send(far, far, CORE)

    def end(self):
        self.near.wait_recv()
        self.far.wait_recv()


class RingReduce:
    def __init__(self, net, up, down, hop_in, last_in, lo, hi):
        self.net, self.up, self.down, self.hop_in, self.last_in = net, up, down, hop_in, last_in
        self.lo, self.hi, self.tail = lo, hi, []

    def far(self, chunk):
        self.a = self.net.send(chunk.at[self.lo], self.hop_in.at[0], self.up)
        self.b = self.net.send(chunk.at[self.hi], self.hop_in.at[1], self.down)

    def put(self, chunk, i, rows, way):
        self.tail.append(self.net.send(chunk.at[rows], self.last_in.at[i].at[rows], way))

    def above_now(self, chunk):
        self.put(chunk, 0, self.hi, self.up)

    def below_now(self, chunk):
        self.put(chunk, 1, self.lo, self.down)

    def above(self, chunk):
        part = chunk.at[self.lo]
        self.a.wait_recv()
        part[...] = (part[...].astype(F32) + self.hop_in[0].astype(F32)).astype(BF)
        self.put(chunk, 0, self.lo, self.up)

    def below(self, chunk):
        part = chunk.at[self.hi]
        self.b.wait_recv()
        part[...] = (part[...].astype(F32) + self.hop_in[1].astype(F32)).astype(BF)
        self.put(chunk, 1, self.hi, self.down)

    def last(self, own):
        own = own.astype(F32)
        for copy in self.tail:
            copy.wait_recv()
        return own + self.last_in[0].astype(F32) + self.last_in[1].astype(F32)


NT = (((1,), (1,)), ((), ()))
TN = (((0,), (0,)), ((), ()))
N_COPIES = 40 * 2 + 7 * 4 * 2 + 14 + 4 + 6 * 9 + 1 + 42 + 6


def kernel(
    x_ref, gout_ref, mod_ref, it_ref, pos_ref, wq_hbm, wo_hbm,
    gin, gmod, gqkv, gow,
    nf, gf, qkvg, wv, wo, wog,
    aq, pq, rq, hq, hqi, oq, iq, ag, pg, rg, hg, hgi, og, ig, mine, got, mine2, got2,
    kv, wts, pos_t, stats, dk, dv, part, part_in,
    gpq, gpkv, cx, gnq, gn, yh0, yi0, t0, zh0, zi0, zh1, zi1, t1, yh1, yi1,
    outq, ow, sums, sums_z, sums_y,
    send_sem, recv_sem, load_sem, store_sem,
):
    x, k, y, z = coords()
    net = Net(send_sem, recv_sem)
    loads = load_weights(wq_hbm, wo_hbm, wv, wo, load_sem)
    enter(OTHERS + [YP, YM, Y2, ZP, ZM, Z2])
    it = it_ref[0]
    shift, scale, gate = [mod_ref[i, pl.ds(it, 1), :] for i in range(3)]

    gf[y, z] = gout_ref[...]
    cot = Gather(net, gf)
    cot.s1()
    xf = x_ref[...].astype(F32)
    squares = RowSum(net, mine, got, jnp.sum(xf * xf, axis=1, keepdims=True))
    pos = [[pos_ref[:, pl.ds(g * 384 + h * HALF, HALF)] for g in range(4)] for h in range(2)]
    key_pos = jnp.concatenate(pos[0] + pos[1], axis=1)
    for g in range(4):
        own_pos = jnp.where(k == 0, pos[0][g], pos[1][g])
        pos_t[g] = jnp.broadcast_to(own_pos, (128, HALF)).T
    inv = lax.rsqrt(squares.total() / D + EPS)
    nf[y, z] = (xf * inv * (1.0 + scale) + shift).astype(BF)
    act = Gather(net, nf)
    act.s1()
    order = (y, (y + 3) % 4, (y + 1) % 4, (y + 2) % 4)
    rows_q = RowReduce(net, aq, pq, rq, hq, hqi, oq, iq, 384)
    rows_g = RowReduce(net, ag, pg, rg, hg, hgi, og, ig, 128)

    def half_of(buf, s, h):
        return buf[order[s], pl.ds(2 * h, 2)].reshape(HALF, 1024)

    def multiply(s):
        for h, dst in ((1 - k, pq), (k, aq)):
            a = half_of(nf, s, h)
            r = jnp.dot(a, wv[:, pl.ds(0, 512)], preferred_element_type=F32).astype(dst.dtype)
            for d in range(4):
                dst[s, :, pl.ds(d * 384, 128)] = r[:, d * 128 : d * 128 + 128]
            r = jnp.dot(a, wv[:, pl.ds(512, 1024)], preferred_element_type=F32).astype(dst.dtype)
            for d in range(4):
                dst[s, :, pl.ds(d * 384 + 128, 256)] = r[:, d * 256 : d * 256 + 256]
            if dst is pq:
                rows_q.start(s)

    def multiply_g(s):
        for h, dst in ((1 - k, pg), (k, ag)):
            r = lax.dot_general(half_of(gf, s, h), wog[...], NT, preferred_element_type=F32)
            dst[s] = r.astype(dst.dtype)
            if dst is pg:
                rows_g.start(s)

    swaps = []

    def finish(s):
        r = rows_q.r3(s)
        qkvg[order[s], :, pl.ds(0, 128)] = r[:, 0:128]
        kv[k, order[s]] = r[:, 128:384]
        half = kv.at[k, order[s]]
        swaps.append(net.send(half, half, CORE))

    def finish_g(s):
        qkvg[order[s], :, pl.ds(128, 128)] = rows_g.r3(s)

    act.s2()
    for copy in loads:
        copy.wait()
    act.s3()
    multiply(0)
    act.s4()
    rows_q.r1(0)
    act.s5()
    multiply(1)
    rows_q.r2(0)
    cot.s2()
    multiply(2)
    rows_q.r1(1)
    act.s6()
    rows_q.r1(2)
    multiply(3)
    rows_q.r2(1)
    cot.s3()
    rows_q.r2(2)
    rows_q.r1(3)
    cot.s4()
    wog[...] = (wo[...].astype(F32) * gate).astype(BF)
    finish(0)
    cot.s5()
    rows_q.r2(3)
    multiply_g(0)
    multiply_g(1)
    finish(1)
    rows_g.r1(0)
    multiply_g(2)
    rows_g.r1(1)
    finish(2)
    cot.s6()
    multiply_g(3)
    rows_g.r1(2)
    rows_g.r2(0)
    finish(3)
    rows_g.r1(3)
    rows_g.r2(1)

    groups = ((y + 2) % 4, (y + 1) % 4, (y + 3) % 4, y)
    for copy in swaps:
        copy.wait_recv()
    keys = kv[:, :, :, pl.ds(0, 128)].reshape(1536, 128)
    values = kv[:, :, :, pl.ds(128, 128)].reshape(1536, 128)
    factor = 1.0 / HEAD_DIM**0.5

    def attend(s):
        q = qkvg[groups[s], :, pl.ds(0, 128)]
        scores = lax.dot_general(q, keys, NT, preferred_element_type=F32)
        scores = jnp.where(key_pos <= pos_t[groups[s], :, pl.ds(0, 1)], scores, -1e30)
        peak = jnp.max(scores, axis=1, keepdims=True)
        weights = jnp.exp2((scores - peak) * (factor * LOG2E))
        wts[s] = weights
        inverse = 1.0 / jnp.sum(weights, axis=1, keepdims=True)
        stats[s] = jnp.broadcast_to(inverse, (HALF, 128))
        probs_b = (weights * inverse).astype(BF)
        r = jnp.dot(probs_b, values, preferred_element_type=F32)
        cx[groups[s], k, :, pl.ds(384, 128)] = r.astype(BF)

    def attend_grad(s):
        q = qkvg[groups[s], :, pl.ds(0, 128)]
        g = qkvg[groups[s], :, pl.ds(128, 128)]
        weights, inverse = wts[s], stats[s, :, pl.ds(0, 1)]
        probs_b = (weights * inverse).astype(BF)
        grad_probs = lax.dot_general(g, values, NT, preferred_element_type=F32)
        delta = jnp.sum(weights * grad_probs, axis=1, keepdims=True) * inverse
        grad_scores = (weights * (grad_probs - delta) * (inverse * factor)).astype(BF)
        r = jnp.dot(grad_scores, keys, preferred_element_type=F32)
        gpq[groups[s], k, :, pl.ds(384, 128)] = r.astype(BF)
        grad_k = jnp.dot(q.T, grad_scores, preferred_element_type=F32)
        grad_v = jnp.dot(g.T, probs_b, preferred_element_type=F32)
        if s == 3:
            dk[...] = grad_k
            dv[...] = grad_v
        else:
            dk[...] += grad_k
            dv[...] += grad_v

    def gather_q(s):
        return RowGather(net, lambda rows, cols: gpq.at[groups[s], k, rows, cols], 128)

    def gather_kv(s):
        return RowGather(net, lambda rows, cols: gpkv.at[groups[s], k, rows, cols], 256)

    moves_q = [gather_q(s) for s in range(4)]
    moves_kv = [gather_kv(s) for s in range(4)]
    context = RowGather(net, lambda rows, cols: cx.at[:, k, rows, cols], 128)

    attend(0)
    rows_g.r2(2)
    attend(1)
    attend(2)
    rows_g.r2(3)
    attend(3)
    for i in range(4):
        finish_g(i)
        attend_grad(3 - i)
        if i < 3:
            moves_q[3 - i].start()
    mine_at = pl.ds(pl.multiple_of(k * 768, 128), 768)
    theirs_at = pl.ds(pl.multiple_of((1 - k) * 768, 128), 768)
    part[pl.ds(0, 128)] = dk[:, theirs_at].astype(BF)
    part[pl.ds(128, 128)] = dv[:, theirs_at].astype(BF)
    swap = net.send(part, part_in, CORE)
    moves_q[0].start()

    stores = []

    def store(src, dst):
        copy = pltpu.make_async_copy(src, dst, store_sem.at[len(stores)])
        copy.start()
        stores.append(copy)

    heads = heads_of(x)
    head_at = [pl.ds(pl.multiple_of(head * 128, 128), 128) for head in heads]
    lo, hi = pl.ds(0, 48), pl.ds(48, 48)
    ring_y0 = RingReduce(net, YP, YM, yh0, yi0, pl.ds(0, 2), pl.ds(2, 2))
    rings_z1 = [RingReduce(net, ZP, ZM, zh1.at[s], zi1.at[s], lo, hi) for s in range(4)]
    ring_z0 = RingReduce(net, ZP, ZM, zh0, zi0, lo, hi)
    ring_y1 = RingReduce(net, YP, YM, yh1, yi1, lo, hi)
    zp, zm, z2 = (z + 1) % 4, (z + 3) % 4, (z + 2) % 4

    def normed_q(s):
        moves_q[s].end()
        a = gpq[groups[s]].reshape(384, 512)
        gnq[s] = lax.dot_general(a, wv[:, pl.ds(0, 512)], NT, preferred_element_type=F32)

    def normed_kv(s):
        moves_kv[s].end()
        a = gpkv[groups[s]].reshape(384, 1024)
        r = lax.dot_general(a, wv[:, pl.ds(512, 1024)], NT, preferred_element_type=F32)
        gn[s] = (gnq[s] + r).astype(BF).reshape(4, 96, 1024)

    def out_weight():
        context.end()
        all_g = gf[...].reshape(1536, 1024)
        gate_grad = jnp.zeros((1, 1024), F32)
        for m in range(2):
            rows = pl.ds(m * 256, 256)
            left = cx[:, :, :, rows].reshape(1536, 256)
            r = lax.dot_general(left, all_g, TN, preferred_element_type=F32)
            gate_grad += jnp.sum(r * wo[rows, :].astype(F32), axis=0, keepdims=True)
            ow[rows, :] = (r * gate).astype(BF)
        for d in range(4):
            store(ow.at[pl.ds(d * 128, 128)], gow.at[head_at[d], :])
        return gate_grad

    def weight_q(m):
        rows = pl.ds(m * 256, 256)
        left = nf[:, :, :, rows].reshape(1536, 256)
        right = gpq[...].reshape(1536, 512)
        r = lax.dot_general(left, right, TN, preferred_element_type=F32)
        outq[rows, pl.ds(0, 512)] = r.astype(BF)

    def weight_kv(m):
        rows = pl.ds(m * 256, 256)
        left = nf[:, :, :, rows].reshape(1536, 256)
        right = gpkv[...].reshape(1536, 1024)
        r = lax.dot_general(left, right, TN, preferred_element_type=F32)
        outq[rows, pl.ds(512, 1024)] = r.astype(BF)

    def z1_far(s):
        rings_z1[s].far(gn.at[s, z2, :, R1])
        rings_z1[s].above_now(gn.at[s, zp, :, R1])
        rings_z1[s].below_now(gn.at[s, zm, :, R1])

    def z1_near(s):
        rings_z1[s].above(gn.at[s, zp, :, R1])
        rings_z1[s].below(gn.at[s, zm, :, R1])

    def z1_last(s):
        return rings_z1[s].last(gn[s, z, :, R1])

    def rows_of(s):
        return gn.at[s, :, :, R0]

    swap.wait_recv()
    for i, total in ((0, dk), (1, dv)):
        r = total[:, mine_at] + part_in[pl.ds(i * 128, 128)].astype(F32)
        gpkv[:, k, :, pl.ds(768 + i * 128, 128)] = r.T.astype(BF).reshape(4, HALF, 128)
    moves_kv[0].start()
    moves_kv[1].start()
    for s in (3, 2, 1, 0):
        moves_q[s].forward()
    moves_kv[0].forward()
    moves_kv[2].start()
    for s in (3, 2, 1, 0):
        moves_q[s].finish()
    moves_kv[1].forward()
    moves_kv[3].start()
    normed_q(0)
    normed_q(1)
    moves_kv[0].finish()
    normed_q(2)
    normed_q(3)
    normed_kv(0)
    ring_y0.far(rows_of(0))
    z1_far(0)
    moves_kv[2].forward()
    moves_kv[1].finish()
    weight_q(0)
    weight_q(1)
    normed_kv(1)
    ring_y0.above_now(rows_of(1))
    z1_far(1)
    moves_kv[3].forward()
    context.start()
    moves_kv[2].finish()
    z1_near(0)
    weight_q(2)
    normed_kv(2)
    ring_y0.below_now(rows_of(2))
    z1_far(2)
    moves_kv[3].finish()
    ring_y0.above(rows_of(1))
    z1_near(1)
    normed_kv(3)
    z1_far(3)
    ring_y0.below(rows_of(2))
    t1[0] = z1_last(0).astype(BF)
    ring_y1.far(t1.at[0])
    z1_near(2)
    context.forward()
    t1[1] = z1_last(1).astype(BF)
    ring_y1.above_now(t1.at[1])
    weight_q(3)
    z1_near(3)
    t0[...] = ring_y0.last(gn[3, :, :, R0]).astype(BF)
    ring_z0.far(t0.at[z2])
    ring_z0.above_now(t0.at[zp])
    ring_z0.below_now(t0.at[zm])
    ring_y1.above(t1.at[1])
    t1[2] = z1_last(2).astype(BF)
    ring_y1.below_now(t1.at[2])
    ring_y1.below(t1.at[2])
    context.finish()
    weight_kv(0)
    weight_kv(1)
    ring_z0.above(t0.at[zp])
    ring_z0.below(t0.at[zm])
    gate_grad = out_weight()
    t1[3] = z1_last(3).astype(BF)

    grad0 = ring_z0.last(t0[z])
    grad1 = ring_y1.last(t1[3])
    grad = jnp.concatenate([grad0, grad1], axis=1)
    x_hat = x_ref[...].astype(F32) * inv
    grad_hat = grad * (1.0 + scale)
    sums[0, pl.ds(0, 1)] = jnp.sum(grad, axis=0, keepdims=True)
    sums[0, pl.ds(1, 1)] = jnp.sum(grad * x_hat, axis=0, keepdims=True)
    sums[0, pl.ds(2, 1)] = gate_grad
    sums[0, pl.ds(3, 5)] = jnp.zeros((5, 1024), F32)
    sums_z[z] = sums[0]
    zc = [net.send(sums.at[0], sums_z.at[z], step) for step in (ZP, ZM, Z2)]
    inner = RowSum(net, mine2, got2, jnp.sum(grad_hat * x_hat, axis=1, keepdims=True))
    weight_kv(2)
    weight_kv(3)
    for d in range(4):
        for j, place in enumerate((d * 128, 512 + d * 256, 640 + d * 256)):
            store(outq.at[:, pl.ds(place, 128)], gqkv.at[j, :, head_at[d]])
    for copy in zc:
        copy.wait_recv()
    sums[1] = (sums_z[0] + sums_z[1]) + (sums_z[2] + sums_z[3])
    sums_y[y] = sums[1]
    yc = [net.send(sums.at[1], sums_y.at[y], step) for step in (YP, YM, Y2)]
    inner = inner.total() / D
    gin[...] = ((grad_hat - x_hat * inner) * inv + gout_ref[...].astype(F32)).astype(BF)
    for copy in yc:
        copy.wait_recv()
    gmod[...] = ((sums_y[0] + sums_y[1]) + (sums_y[2] + sums_y[3]))[0:3]
    net.drain()
    for copy in stores:
        copy.wait()


def place_kernel(a, b, c, d, oa, ob, oc, od, va, vb_, vc, vd, load_sem, store_sem):
    parts = []
    for src, mid, dst, n in ((a, va, oa, 1), (b, vb_, ob, 1), (c, vc, oc, 6), (d, vd, od, 2)):
        for i in range(n):
            if n == 6:
                at = (i // 2, pl.ds(512 * (i % 2), 512))
            elif n == 2:
                at = (pl.ds(256 * i, 256),)
            else:
                at = (slice(None),)
            parts.append((src.at[at], mid.at[at], dst.at[at]))
    loads = [pltpu.make_async_copy(p[0], p[1], load_sem.at[i]) for i, p in enumerate(parts)]
    puts = [pltpu.make_async_copy(p[1], p[2], store_sem.at[i]) for i, p in enumerate(parts)]
    for copy in loads:
        copy.start()
    for load, put in zip(loads, puts):
        load.wait()
        put.start()
    for copy in puts:
        copy.wait()


VM = pl.BlockSpec(memory_space=pltpu.VMEM)
SM = pl.BlockSpec(memory_space=pltpu.SMEM)
ANY = pl.BlockSpec(memory_space=pl.ANY)


def vb(*shape):
    return pltpu.VMEM(shape, BF)


def vf(*shape):
    return pltpu.VMEM(shape, F32)


def sds(shape, dtype=BF):
    return jax.ShapeDtypeStruct(shape, dtype)


def shards(block_input, modulation, iteration, positions, qkv_weight, out_weight, grad_out):
    mod = modulation.transpose(1, 0, 2)
    wq = qkv_weight.transpose(1, 0, 2)
    pos = positions.reshape(1, 1536)

    def rows(w):
        return [
            vf(4, HALF, 4 * w), vb(4, HALF, 4 * w), vb(4, HALF, 4 * w), vb(4, HALF, w),
            vb(4, 2, 96, w), vb(4, 2, HALF, w), vb(4, 2, HALF, w),
        ]

    gin, gmod, gqkv, gow = pl.pallas_call(
        kernel,
        name="block_backward",
        out_shape=(sds((96, 1024)), sds((3, 1024), F32), sds((3, 1024, 512)), sds((512, 1024))),
        in_specs=[VM, VM, VM, SM, VM, ANY, ANY],
        out_specs=(VM, VM, ANY, ANY),
        scratch_shapes=[
            vb(4, 4, 96, 1024), vb(4, 4, 96, 1024), vb(4, HALF, 256),
            vb(1024, 1536), vb(512, 1024), vb(512, 1024),
            *rows(384), *rows(128), vf(8, 128), vf(7, 8, 128), vf(8, 128), vf(7, 8, 128),
            vb(2, 4, HALF, 256), vf(4, HALF, 1536), pltpu.VMEM((4, HALF, 128), jnp.int32), vf(4, HALF, 128),
            vf(128, 1536), vf(128, 1536), vb(256, 768), vb(256, 768),
            vb(4, 2, HALF, 512), vb(4, 2, HALF, 1024), vb(4, 2, HALF, 512),
            vf(4, 384, 1024), vb(4, 4, 96, 1024),
            vb(2, 2, 96, 384), vb(2, 4, 96, 384), vb(4, 96, 384), vb(2, 48, 384), vb(2, 96, 384),
            vb(4, 2, 48, 640), vb(4, 2, 96, 640), vb(4, 96, 640), vb(2, 48, 640), vb(2, 96, 640),
            vb(1024, 1536), vb(512, 1024), vf(2, 8, 1024), vf(4, 8, 1024), vf(4, 8, 1024),
            pltpu.SemaphoreType.DMA((N_COPIES,)), pltpu.SemaphoreType.DMA((N_COPIES,)),
            pltpu.SemaphoreType.DMA((16,)), pltpu.SemaphoreType.DMA((16,)),
        ],
        compiler_params=pltpu.CompilerParams(
            collective_id=0, has_side_effects=True, vmem_limit_bytes=63 << 20
        ),
    )(block_input, grad_out, mod, iteration, pos, wq, out_weight)
    shapes = [(96, 1024), (3, 1024), (3, 1024, 512), (512, 1024)]
    types = [BF, F32, BF, BF]
    gin, gmod, gqkv, gow = pl.pallas_call(
        place_kernel,
        name="place",
        out_shape=[sds(a, b) for a, b in zip(shapes, types)],
        in_specs=[ANY] * 4,
        out_specs=[ANY] * 4,
        scratch_shapes=[pltpu.VMEM(a, b) for a, b in zip(shapes, types)]
        + [pltpu.SemaphoreType.DMA((10,)), pltpu.SemaphoreType.DMA((10,))],
        compiler_params=pltpu.CompilerParams(vmem_limit_bytes=63 << 20),
    )(gin, gmod, gqkv, gow)
    return gin, gqkv.transpose(1, 0, 2), gow, gmod


def solution(mesh):
    placed = (
        P("col", "row"),
        P(None, None, "row"),
        P(),
        P(),
        P("row", None, "col"),
        P("col", "row"),
        P("col", "row"),
    )
    return jax.shard_map(
        shards,
        mesh=mesh,
        in_specs=placed,
        out_specs=(P("col", "row"), P("row", None, "col"), P("col", "row"), P(None, "row")),
        check_vma=False,
    )
```
